1024 devices in a mesh: dom: 128 (over z, y, core), rep: 8 (over x).
Axes of the slice: x: 8, y: 8, z: 8, core: 2. Of those that a mesh axis runs over, the one named last changes fastest.
Arguments:
- features: bfloat16 [262144, 256], P(('dom', 'rep')), may hold values from -6 to 6
- weight: bfloat16 [256, 172], replicated, may hold values from -0.375 to 0.375
- tiles: bfloat16 [65536, 128, 128], P(('dom', 'rep')), may hold values from -0.09375 to 0.09375
- tile_rows: int32 [65536], P(('dom', 'rep')), may hold values from 0 to 1
- tile_cols: int32 [65536], P(('dom', 'rep')), may hold values from 0 to 23
- send_lists: int32 [2048, 64], P(('dom', 'rep')), may hold values from 0 to 255
- counts: int32 [2048], P(('dom', 'rep')), may hold values from 1 to 64, as said below
- labels: int32 [262144], P(('dom', 'rep')), may hold values from 0 to 171
Outputs:
- grad_features: bfloat16 [262144, 256], P(('dom', 'rep'))
- grad_weight: float32 [256, 172], replicated
- loss: float32 [], replicated
The draws below stay inside these ranges and needn't reach their ends.
Inputs may be any that keep to these rules, and one draw needn't show every extreme that they name: `counts`: at most 64, and a list of 64 live slots occurs in every draw.
All inputs are finite; a program needn't handle non-finite values.
Results may differ from the reference program's by a relative error of at most 0.0055.
Values may be sent and summed in bfloat16 or wider, within the bound.
No kernel may reach another device: no remote copies, remote signals or barrier semaphores. Data moves between devices by JAX's collectives and lax.ppermute only.
A program may use at most 32 MiB of HBM per device.

```python
import jax
import jax.numpy as jnp
from jax import lax

H = 256
C = 172
TB = 128
NODE_DEV = 256
TILES = 64
SEND = 64
NODES = 262144
SLOTS = 2048
COLT = 24
N_DOM = 128
N_REP = 8


def draw_counts(key, part):
    key = jax.random.fold_in(key, 5)
    first_key, second_key = jax.random.split(key)
    first = jax.random.randint(first_key, (SLOTS,), 0, SEND + 1)
    second = jax.random.randint(second_key, (SLOTS,), 0, SEND + 1)
    values = jnp.maximum(first * second // SEND, 1)
    return values.at[0].set(SEND).astype(jnp.int32)


def plant(array, key, smallest, top_value):
    place = [jax.random.randint(jax.random.fold_in(key, axis), (), 0, length) for axis, length in enumerate(array.shape)]
    main_axis = array.shape.index(max(array.shape))
    beside = place[:main_axis] + [(place[main_axis] + 1) % array.shape[main_axis]] + place[main_axis + 1:]
    return array.at[tuple(place)].set(smallest).at[tuple(beside)].set(top_value)


def steps_of(key, extent, cuts, low, top_value):
    level = 1.0
    for position, blocks in cuts:
        draws = jax.random.uniform(jax.random.fold_in(jax.random.fold_in(key, 6), position), (blocks,), jnp.float32, low / len(cuts), top_value / len(cuts))
        level = level * jnp.repeat(jnp.exp(draws), extent[position] // blocks).reshape((-1,) + (1,) * (len(extent) - 1 - position))
    return level


def centred(stream_key, dims, spread, limit, cuts=(), kind=jnp.bfloat16):
    drawn = spread * jax.random.normal(stream_key, dims, jnp.float32)
    if cuts:
        drawn = drawn * steps_of(stream_key, dims, cuts, -0.22, 0.18)
    return jnp.clip(drawn, -limit, limit).astype(kind)


def setup_inputs(seed: int = 0) -> dict:
    seeds = jax.random.split(jax.random.key(seed), 9)
    return {
        "features": centred(seeds[0], (NODES, H), 1.0, 6.0, ((0, 1024),)),
        "weight": centred(seeds[1], (H, C), H ** -0.5, 0.375),
        "tiles": centred(seeds[2], (N_DOM * N_REP * TILES, TB, TB), (TILES * TB * TB // NODE_DEV) ** -0.5, 0.09375, ((0, 1024),)),
        "tile_rows": plant(jax.random.randint(seeds[3], (N_DOM * N_REP * TILES,), 0, NODE_DEV // TB), jax.random.fold_in(seeds[3], 1), 0, (NODE_DEV // TB) - 1).astype(jnp.int32),
        "tile_cols": plant(jax.random.randint(seeds[4], (N_DOM * N_REP * TILES,), 0, COLT), jax.random.fold_in(seeds[4], 1), 0, COLT - 1).astype(jnp.int32),
        "send_lists": plant(jax.random.randint(seeds[5], (SLOTS, SEND), 0, NODE_DEV), jax.random.fold_in(seeds[5], 1), 0, NODE_DEV - 1).astype(jnp.int32),
        "counts": draw_counts(jax.random.fold_in(seeds[8], 71), 0),
        "labels": plant(jax.random.randint(seeds[7], (NODES,), 0, C), jax.random.fold_in(seeds[7], 1), 0, C - 1).astype(jnp.int32),
    }


def partition(inputs):
    ext_d, tiles_d, rows_d, cols_d, labels_d = inputs
    cols_view = ext_d.reshape(-1, TB, C).astype(jnp.float32)

    def member(carry, item):
        column_grads, total = carry
        tile_set, rows, cols, lab = item
        tile_f = tile_set.astype(jnp.float32)
        chosen = cols_view[cols]
        products = jnp.einsum('tij,tjc->tic', tile_f, chosen)
        logits = jnp.zeros((NODE_DEV // TB, TB, C), jnp.float32).at[rows].add(products).reshape(NODE_DEV, C)
        peak = jnp.max(logits, axis=1, keepdims=True)
        shifted = logits - peak
        logp = shifted - jnp.log(jnp.sum(jnp.exp(shifted), axis=1, keepdims=True))
        onehot = lab[:, None] == jnp.arange(C, dtype=jnp.int32)[None, :]
        total = total - jnp.sum(jnp.where(onehot, logp, jnp.float32(0.0)))
        grad_logits = (jnp.exp(logp) - onehot.astype(jnp.float32)).astype(jnp.bfloat16)
        grad_tiles = grad_logits.reshape(NODE_DEV // TB, TB, C)[rows].astype(jnp.float32)
        parts = jnp.einsum('tji,tjc->tic', tile_f, grad_tiles)
        column_grads = column_grads.at[cols].add(parts)
        return (column_grads, total), None

    init = (jnp.zeros((COLT, TB, C), jnp.float32), jnp.float32(0.0))
    (column_grads, total), _ = lax.scan(member, init, (tiles_d, rows_d, cols_d, labels_d))
    return column_grads.reshape(N_REP, NODE_DEV + 2 * SEND, C), total


def reference(features, weight, tiles, tile_rows, tile_cols, send_lists, counts, labels):
    block = NODE_DEV + 2 * SEND
    projected = jnp.dot(features, weight, preferred_element_type=jnp.float32).astype(jnp.bfloat16)
    proj = projected.reshape(N_DOM, N_REP, NODE_DEV, C)
    lists = send_lists.reshape(N_DOM, N_REP, 2, SEND)
    live = jnp.arange(SEND, dtype=jnp.int32)[None, None, None, :] < counts.reshape(N_DOM, N_REP, 2)[..., None]
    picked = jnp.take_along_axis(proj[:, :, None, :, :], lists[..., None], axis=3)
    picked = jnp.where(live[..., None], picked, jnp.zeros_like(picked))
    zero = jnp.zeros_like(picked[:1, :, 0])
    from_left = jnp.concatenate([zero, picked[:-1, :, 1]], axis=0)
    from_right = jnp.concatenate([picked[1:, :, 0], zero], axis=0)
    extended = jnp.concatenate([proj, from_left, from_right], axis=2).reshape(N_DOM, N_REP * block, C)
    column_grads, totals = lax.map(partition, (
        extended,
        tiles.reshape(N_DOM, N_REP, TILES, TB, TB),
        tile_rows.reshape(N_DOM, N_REP, TILES),
        tile_cols.reshape(N_DOM, N_REP, TILES),
        labels.reshape(N_DOM, N_REP, NODE_DEV)))
    own = column_grads[:, :, :NODE_DEV]
    grad_left = column_grads[:, :, NODE_DEV:NODE_DEV + SEND]
    grad_right = column_grads[:, :, NODE_DEV + SEND:]
    fzero = jnp.zeros_like(grad_left[:1])
    back_first = jnp.concatenate([fzero, grad_right[:-1]], axis=0)
    back_second = jnp.concatenate([grad_left[1:], fzero], axis=0)
    mask_first = live[:, :, 0, :, None].astype(jnp.float32)
    mask_second = live[:, :, 1, :, None].astype(jnp.float32)

    def add_back(own_rows, list_first, list_second, first, second):
        return own_rows.at[list_first].add(first).at[list_second].add(second)

    grad_rows = jax.vmap(jax.vmap(add_back))(own, lists[:, :, 0], lists[:, :, 1], back_first * mask_first, back_second * mask_second)
    grad_rows = grad_rows.reshape(NODES, C).astype(jnp.bfloat16)
    grad_features = jnp.dot(grad_rows, weight.T, preferred_element_type=jnp.float32).astype(jnp.bfloat16)
    grad_weight = jnp.dot(features.T, grad_rows, preferred_element_type=jnp.float32) / NODES
    loss = jnp.sum(totals) / NODES
    return grad_features, grad_weight, loss
```

```python
import jax
import jax.numpy as jnp
from jax import lax
from jax.experimental import pallas as pl
from jax.experimental.pallas import tpu as pltpu
from jax.sharding import Mesh, PartitionSpec as P

F32 = jnp.float32
BF16 = jnp.bfloat16
LANES = 128
SHAPE = (8, 8, 2, 8)
LAST = (((1,), (1,)), ((), ()))
FIRST = (((0,), (0,)), ((), ()))
PLAIN = (((1,), (0,)), ((), ()))


def round_up(value, unit):
    return -(-value // unit) * unit


def dot(a, b, dims=PLAIN):
    return lax.dot_general(a, b, dims, preferred_element_type=F32)


def vmem():
    return pl.BlockSpec(memory_space=pltpu.VMEM)


def smem():
    return pl.BlockSpec(memory_space=pltpu.SMEM)


def params(mib):
    return pltpu.CompilerParams(vmem_limit_bytes=mib * 2**20)


def pick_kernel(lists, features, picked):
    rows, slots = features.shape[0], lists.shape[1]
    chosen = lax.broadcasted_iota(jnp.int32, (rows, slots), 0) == lists[...]
    onehot = jnp.where(chosen, 1.0, 0.0).astype(BF16)
    picked[...] = dot(onehot, features[...], FIRST).astype(BF16)


def layer_kernel(rows, cols, tiles, columns, weight, labels, out, sums, grads):
    count, tile = tiles.shape[0], tiles.shape[1]
    classes, hidden = weight.shape
    padded = grads.shape[1]
    nodes = labels.shape[1]
    group = 4

    def masked(t):
        block = tiles[t]
        none = jnp.zeros_like(block)
        first = rows[t] == 0
        return jnp.where(first, block, none), jnp.where(first, none, block)

    sums[...] = jnp.zeros_like(sums)
    for start in range(0, count, group):
        picks = [masked(t) for t in range(start, start + group)]
        left = jnp.concatenate(
            [jnp.concatenate([p[i] for p in picks], axis=1) for i in range(2)], axis=0
        )
        right = jnp.concatenate([columns[cols[t]] for t in range(start, start + group)], axis=0)
        sums[...] += dot(left, right)

    total = sums[...]
    high = total.astype(BF16)
    low = (total - high.astype(F32)).astype(BF16)
    wide = jnp.concatenate(
        [weight[...].astype(F32), jnp.zeros((padded - classes, hidden), F32)], axis=0
    ).astype(BF16)
    logits = dot(wide, high, LAST) + dot(wide, low, LAST)
    kind = lax.broadcasted_iota(jnp.int32, (padded, nodes), 0)
    real = kind < classes
    logits = jnp.where(real, logits, -jnp.inf)
    shifted = logits - jnp.max(logits, axis=0, keepdims=True)
    logp = shifted - jnp.log(jnp.sum(jnp.exp(shifted), axis=0, keepdims=True))
    onehot = kind == labels[...]
    losses = -jnp.sum(jnp.where(onehot, logp, 0.0), axis=0, keepdims=True)
    grad = (jnp.exp(logp) - onehot.astype(F32)).astype(BF16)

    weight_grad = dot(grad, high) + dot(grad, low)
    weight_grad = jnp.where(kind == classes, losses, weight_grad)
    quarter = out.shape[1] - 3 * padded
    weight_grad = jnp.concatenate(
        [weight_grad, jnp.zeros((4 * quarter - padded, hidden), F32)], axis=0
    ).astype(BF16)
    for r in range(8):
        h, q = r // 4, r % 4
        out[r, 3 * padded :, :] = weight_grad[
            q * quarter : (q + 1) * quarter, h * LANES : (h + 1) * LANES
        ]

    grads[...] = jnp.zeros_like(grads)
    for start in range(0, count, 2):
        a, b = masked(start), masked(start + 1)
        right = jnp.concatenate(
            [jnp.concatenate([a[i], b[i]], axis=1) for i in range(2)], axis=0
        )
        both = dot(grad, right)
        grads[cols[start]] += both[:, :tile]
        grads[cols[start + 1]] += both[:, tile:]
    for r in range(8):
        for j in range(3):
            out[r, j * padded : (j + 1) * padded, :] = grads[3 * r + j].astype(BF16)


def fold_kernel(parts, own, halo, chunk):
    padded = halo.shape[0]
    summed = parts[0].astype(F32)
    for k in range(1, parts.shape[0]):
        summed += parts[k].astype(F32)
    own[...] = summed[: 2 * padded]
    halo[...] = summed[2 * padded : 3 * padded].astype(BF16)
    chunk[...] = jnp.broadcast_to(summed[3 * padded :][None], chunk.shape)


def sum_kernel(parts, out):
    summed = parts[0]
    for k in range(1, parts.shape[0]):
        summed += parts[k]
    out[...] = jnp.broadcast_to(summed[None], out.shape)


def pair_kernel(a, b, out):
    out[...] = jnp.broadcast_to((a[...] + b[...])[None], out.shape)


def rows_kernel(own, before, after, lists, weight, out):
    padded = before.shape[0]
    classes, hidden = weight.shape
    nodes, slots = out.shape[0], lists.shape[1]
    send = slots // 2
    chosen = lax.broadcasted_iota(jnp.int32, (nodes, slots), 0) == lists[...]
    onehot = jnp.where(chosen, 1.0, 0.0).astype(BF16)
    low = lax.broadcasted_iota(jnp.int32, (padded, slots), 1)
    back = jnp.where(low < send, pltpu.roll(before[...].astype(F32), send, 1), pltpu.roll(after[...].astype(F32), send, 1))
    total = jnp.concatenate([own[:padded], own[padded:]], axis=1)
    total += dot(back.astype(BF16), onehot, LAST)
    grad = total[:classes].astype(BF16)
    out[...] = dot(grad, weight[...], FIRST).astype(BF16)


def last_kernel(parts, weight_grad, loss, scale):
    classes = weight_grad.shape[0]
    gathered = jnp.concatenate(
        [jnp.concatenate([parts[4 * h + q] for q in range(4)], axis=0) for h in range(2)], axis=1
    )
    weight_grad[...] = gathered[:classes] * scale
    loss[...] = jnp.sum(gathered[classes : classes + 1], axis=1, keepdims=True) * scale


def per_device(features, weight, tiles, tile_rows, tile_cols, send_lists, counts, labels):
    nodes, hidden = features.shape
    classes = weight.shape[1]
    send = send_lists.shape[1]
    slots = 2 * send
    tile = tiles.shape[1]
    reps = lax.axis_size("x")
    domains = lax.axis_size("z") * lax.axis_size("y") * lax.axis_size("c")
    padded = round_up(classes + 1, 16)
    quarter = round_up(-(-padded // 4), 16)
    height = 3 * padded + quarter
    dom = ("z", "y", "c")
    up = [(i, i + 1) for i in range(domains - 1)]
    down = [(i + 1, i) for i in range(domains - 1)]
    shape = jax.ShapeDtypeStruct
    weight = weight.T

    live = jnp.arange(send, dtype=jnp.int32)[None, :] < counts[:, None]
    lists = jnp.where(live, send_lists, -1).reshape(1, slots)
    picked = pl.pallas_call(
        pick_kernel,
        out_shape=shape((slots, hidden), BF16),
        in_specs=[vmem()] * 2,
        out_specs=vmem(),
    )(lists, features)
    from_before = lax.ppermute(picked[send:], dom, up)
    from_after = lax.ppermute(picked[:send], dom, down)
    block = jnp.concatenate([features, from_before, from_after], axis=0)
    extended = lax.all_gather(block, "x", axis=0, tiled=True)

    payload = pl.pallas_call(
        layer_kernel,
        out_shape=shape((reps, height, LANES), BF16),
        in_specs=[smem(), smem(), vmem(), vmem(), vmem(), vmem()],
        out_specs=vmem(),
        scratch_shapes=[
            pltpu.VMEM((nodes, hidden), F32),
            pltpu.VMEM((3 * reps, padded, tile), F32),
        ],
        compiler_params=params(40),
    )(
        tile_rows,
        tile_cols,
        tiles,
        extended.reshape(-1, tile, hidden),
        weight,
        labels.reshape(1, nodes),
    )
    parts = lax.all_to_all(payload, "x", 0, 0, tiled=True)
    own, halo, chunk = pl.pallas_call(
        fold_kernel,
        out_shape=(
            shape((2 * padded, LANES), F32),
            shape((padded, LANES), BF16),
            shape((lax.axis_size("y"), quarter, LANES), F32),
        ),
        in_specs=[vmem()],
        out_specs=(vmem(),) * 3,
    )(parts)
    before = lax.ppermute(halo, dom, up)
    after = lax.ppermute(halo, dom, down)

    def fold(x, axis, copies):
        return pl.pallas_call(
            sum_kernel,
            out_shape=shape((copies, *x.shape[1:]), F32),
            in_specs=[vmem()],
            out_specs=vmem(),
        )(lax.all_to_all(x, axis, 0, 0, tiled=True))

    chunk = fold(fold(chunk, "y", lax.axis_size("z")), "z", 1)[0]
    other = lax.ppermute(chunk, "c", [(0, 1), (1, 0)])
    chunk = pl.pallas_call(
        pair_kernel,
        out_shape=shape((reps, quarter, LANES), F32),
        in_specs=[vmem()] * 2,
        out_specs=vmem(),
    )(chunk, other)
    chunks = lax.all_to_all(chunk, "x", 0, 0, tiled=True)
    scale = 1.0 / (domains * reps * nodes)
    weight_grad, loss = pl.pallas_call(
        lambda a, b, c: last_kernel(a, b, c, scale),
        out_shape=(shape((classes, hidden), F32), shape((1, 1), F32)),
        in_specs=[vmem()],
        out_specs=(vmem(),) * 2,
    )(chunks)

    grad_features = pl.pallas_call(
        rows_kernel,
        out_shape=shape((nodes, hidden), BF16),
        in_specs=[vmem()] * 5,
        out_specs=vmem(),
    )(own, before, after, lists, weight)
    return grad_features, weight_grad.T, loss.reshape(())


def solution(mesh):
    split = Mesh(mesh.devices.reshape(SHAPE), ("z", "y", "c", "x"))
    both = ("z", "y", "c", "x")
    placed = (
        P(both, None),
        P(),
        P(both, None, None),
        P(both),
        P(both),
        P(both, None),
        P(both),
        P(both),
    )
    return jax.shard_map(
        per_device,
        mesh=split,
        in_specs=placed,
        out_specs=(P(both, None), P(), P()),
        check_vma=False,
    )
```

```python
import jax
import jax.numpy as jnp
from jax import lax
from jax.experimental import pallas as pl
from jax.experimental.pallas import tpu as pltpu
from jax.sharding import Mesh, PartitionSpec as P

F32 = jnp.float32
BF16 = jnp.bfloat16
LANES = 128
SHAPE = (8, 8, 2, 8)
LAST = (((1,), (1,)), ((), ()))
FIRST = (((0,), (0,)), ((), ()))
PLAIN = (((1,), (0,)), ((), ()))


def round_up(value, unit):
    return -(-value // unit) * unit


def dot(a, b, dims=PLAIN):
    return lax.dot_general(a, b, dims, preferred_element_type=F32)


def vmem():
    return pl.BlockSpec(memory_space=pltpu.VMEM)


def smem():
    return pl.BlockSpec(memory_space=pltpu.SMEM)


def hbm():
    return pl.BlockSpec(memory_space=pl.ANY)


def params(mib):
    return pltpu.CompilerParams(vmem_limit_bytes=mib * 2**20)


def slots_onehot(counts, send_lists, rows):
    send = send_lists.shape[1]
    row = lax.broadcasted_iota(jnp.int32, (rows, send), 0)
    slot = lax.broadcasted_iota(jnp.int32, (rows, send), 1)
    sides = [
        jnp.where((row == send_lists[i : i + 1, :]) & (slot < counts[i]), 1.0, 0.0)
        for i in range(2)
    ]
    return [side.astype(BF16) for side in sides]


def pick_kernel(counts, send_lists, features, first, second):
    sides = slots_onehot(counts, send_lists, features.shape[0])
    for onehot, out in zip(sides, (first, second), strict=True):
        out[...] = dot(onehot, features[...], FIRST).astype(BF16)


def layer_kernel(
    rows, cols, tiles_hbm, own_hbm, halo_hbm, weight, labels,
    weight_out, grads,
    tiles, columns, sums, sems,
):
    count, tile = tiles.shape[0], tiles.shape[1]
    classes, hidden = weight.shape
    padded = grads.shape[1]
    nodes = labels.shape[1]
    group = 4
    copies = [
        pltpu.make_async_copy(own_hbm, columns.at[:, 0:2], sems.at[0]),
        pltpu.make_async_copy(halo_hbm, columns.at[:, 2:3], sems.at[1]),
        pltpu.make_async_copy(tiles_hbm, tiles, sems.at[2]),
    ]
    for copy in copies:
        copy.start()

    def masked(t):
        block = tiles[t]
        none = jnp.zeros_like(block)
        first = rows[t] == 0
        return jnp.where(first, block, none), jnp.where(first, none, block)

    def column(t):
        member = cols[t] // 3
        return columns[member, cols[t] - 3 * member]

    sums[...] = jnp.zeros_like(sums)
    grads[...] = jnp.zeros_like(grads)
    for copy in copies:
        copy.wait()
    for start in range(0, count, group):
        picks = [masked(t) for t in range(start, start + group)]
        left = jnp.concatenate(
            [jnp.concatenate([p[i] for p in picks], axis=1) for i in range(2)], axis=0
        )
        right = jnp.concatenate([column(t) for t in range(start, start + group)], axis=0)
        sums[...] += dot(left, right)

    total = sums[...]
    high = total.astype(BF16)
    low = (total - high.astype(F32)).astype(BF16)
    wide = jnp.concatenate(
        [weight[...].astype(F32), jnp.zeros((padded - classes, hidden), F32)], axis=0
    ).astype(BF16)
    logits = dot(wide, high, LAST) + dot(wide, low, LAST)
    kind = lax.broadcasted_iota(jnp.int32, (padded, nodes), 0)
    logits = jnp.where(kind < classes, logits, -jnp.inf)
    shifted = logits - jnp.max(logits, axis=0, keepdims=True)
    logp = shifted - jnp.log(jnp.sum(jnp.exp(shifted), axis=0, keepdims=True))
    onehot = kind == labels[...]
    losses = -jnp.sum(jnp.where(onehot, logp, 0.0), axis=0, keepdims=True)
    grad = (jnp.exp(logp) - onehot.astype(F32)).astype(BF16)

    weight_grad = dot(grad, high) + dot(grad, low)
    weight_grad = jnp.where(kind == classes, losses, weight_grad)
    pieces, height = weight_out.shape[0] // 2, weight_out.shape[1]
    weight_grad = jnp.concatenate(
        [weight_grad, jnp.zeros((pieces * height - padded, hidden), F32)], axis=0
    )
    for half in range(2):
        for q in range(pieces):
            weight_out[pieces * half + q] = weight_grad[
                q * height : (q + 1) * height, half * LANES : (half + 1) * LANES
            ]

    for start in range(0, count, 2):
        a, b = masked(start), masked(start + 1)
        right = jnp.concatenate([jnp.concatenate([a[i], b[i]], axis=1) for i in range(2)], axis=0)
        both = dot(grad, right)
        grads[cols[start]] += both[:, :tile]
        grads[cols[start + 1]] += both[:, tile:]

def sum_kernel(parts, out):
    summed = parts[0]
    for k in range(1, parts.shape[0]):
        summed += parts[k]
    out[...] = jnp.broadcast_to(summed[None], out.shape)


def rows_kernel(counts, send_lists, own, before, after, weight, out):
    padded = before.shape[0]
    classes = weight.shape[0]
    first, second = slots_onehot(counts, send_lists, out.shape[0])
    send = send_lists.shape[1]
    total = jnp.concatenate([own[0], own[1]], axis=1)
    total += dot(before[:, send:], first, LAST)
    total += dot(after[:, :send], second, LAST)
    grad = total[:classes].astype(BF16)
    out[...] = dot(grad, weight[...], FIRST).astype(BF16)


def last_kernel(scale, parts, weight_grad, loss):
    classes = weight_grad.shape[0]
    pieces = parts.shape[0] // 2
    gathered = jnp.concatenate(
        [
            jnp.concatenate([parts[pieces * h + q] for q in range(pieces)], axis=0)
            for h in range(2)
        ],
        axis=1,
    )
    weight_grad[...] = gathered[:classes] * scale
    loss[...] = jnp.sum(gathered[classes : classes + 1], axis=1, keepdims=True) * scale


def per_device(features, weight, tiles, tile_rows, tile_cols, send_lists, counts, labels):
    nodes, hidden = features.shape
    classes = weight.shape[1]
    send = send_lists.shape[1]
    count, tile = tiles.shape[0], tiles.shape[1]
    reps = lax.axis_size("x")
    dom = ("z", "y", "c")
    domains = lax.axis_size(dom)
    near = ("y", "c")
    pieces = lax.axis_size(near)
    padded = round_up(classes + 1, 16)
    height = round_up(-(-padded // (pieces // 2)), 8)
    up = [(i, i + 1) for i in range(domains - 1)]
    down = [(i + 1, i) for i in range(domains - 1)]
    shape = jax.ShapeDtypeStruct
    weight = weight.T

    first, second = pl.pallas_call(
        pick_kernel,
        out_shape=(shape((send, hidden), BF16),) * 2,
        in_specs=[smem(), vmem(), vmem()],
        out_specs=(vmem(),) * 2,
    )(counts, send_lists, features)
    from_before = lax.ppermute(second, dom, up)
    from_after = lax.ppermute(first, dom, down)
    own_rows = lax.all_gather(features, "x", axis=0, tiled=True)
    halo_rows = lax.all_gather(
        jnp.concatenate([from_before, from_after], axis=0), "x", axis=0, tiled=True
    )

    weight_parts, parts = pl.pallas_call(
        layer_kernel,
        out_shape=(
            shape((pieces, height, LANES), F32),
            shape((3 * reps, padded, tile), F32),
        ),
        in_specs=[smem(), smem(), hbm(), hbm(), hbm(), vmem(), vmem()],
        out_specs=(vmem(),) * 2,
        scratch_shapes=[
            pltpu.VMEM((count, tile, tile), BF16),
            pltpu.VMEM((reps, 3, tile, hidden), BF16),
            pltpu.VMEM((nodes, hidden), F32),
            pltpu.SemaphoreType.DMA((3,)),
        ],
        compiler_params=params(56),
    )(
        tile_rows,
        tile_cols,
        tiles,
        own_rows.reshape(reps, 2, tile, hidden),
        halo_rows.reshape(reps, 1, tile, hidden),
        weight,
        labels.reshape(1, nodes),
    )

    def fold(parts, copies):
        return pl.pallas_call(
            sum_kernel,
            out_shape=shape((copies, *parts.shape[1:]), F32),
            in_specs=[vmem()],
            out_specs=vmem(),
        )(parts)

    weight_parts = lax.all_to_all(weight_parts, near, 0, 0, tiled=True)
    own = lax.psum_scatter(parts, "x", scatter_dimension=0, tiled=True)
    for axis, following in (("z", "z"), ("x", "x"), (near, near)):
        weight_parts = fold(weight_parts, lax.axis_size(axis))
        weight_parts = lax.all_to_all(weight_parts, following, 0, 0, tiled=True)

    halo = own[2].astype(BF16)
    before = lax.ppermute(halo, dom, up)
    after = lax.ppermute(halo, dom, down)
    grad_features = pl.pallas_call(
        rows_kernel,
        out_shape=shape((nodes, hidden), BF16),
        in_specs=[smem()] + [vmem()] * 5,
        out_specs=vmem(),
    )(counts, send_lists, own, before, after, weight)

    scale = 1.0 / (domains * reps * nodes)
    weight_grad, loss = pl.pallas_call(
        lambda *refs: last_kernel(scale, *refs),
        out_shape=(shape((classes, hidden), F32), shape((1, 1), F32)),
        in_specs=[vmem()],
        out_specs=(vmem(),) * 2,
    )(weight_parts)
    return grad_features, weight_grad.T, loss.reshape(())


def solution(mesh):
    split = Mesh(mesh.devices.reshape(SHAPE), ("z", "y", "c", "x"))
    both = ("z", "y", "c", "x")
    placed = (
        P(both, None),
        P(),
        P(both, None, None),
        P(both),
        P(both),
        P(both, None),
        P(both),
        P(both),
    )
    return jax.shard_map(
        per_device,
        mesh=split,
        in_specs=placed,
        out_specs=(P(both, None), P(), P()),
        check_vma=False,
    )
```

```python
import jax
import jax.numpy as jnp
from jax import lax
from jax.experimental import pallas as pl
from jax.experimental.pallas import tpu as pltpu
from jax.sharding import Mesh, PartitionSpec as P

F32 = jnp.float32
BF16 = jnp.bfloat16
LANES = 128
PIECE = 16
SHAPE = (4, 2, 8, 2, 8)
AXES = ("zh", "zl", "y", "c", "x")
LAST = (((1,), (1,)), ((), ()))
FIRST = (((0,), (0,)), ((), ()))
PLAIN = (((1,), (0,)), ((), ()))


def round_up(value, unit):
    return -(-value // unit) * unit


def dot(a, b, dims=PLAIN):
    return lax.dot_general(a, b, dims, preferred_element_type=F32)


def vmem():
    return pl.BlockSpec(memory_space=pltpu.VMEM)


def smem():
    return pl.BlockSpec(memory_space=pltpu.SMEM)


def hbm():
    return pl.BlockSpec(memory_space=pl.ANY)


def params(mib):
    return pltpu.CompilerParams(vmem_limit_bytes=mib * 2**20)


def slots_onehot(counts, send_lists, rows):
    send = send_lists.shape[1]
    row = lax.broadcasted_iota(jnp.int32, (rows, send), 0)
    slot = lax.broadcasted_iota(jnp.int32, (rows, send), 1)
    sides = [
        jnp.where((row == send_lists[i : i + 1, :]) & (slot < counts[i]), 1.0, 0.0)
        for i in range(2)
    ]
    return [side.astype(BF16) for side in sides]


def pick_kernel(counts, send_lists, features, first, second):
    sides = slots_onehot(counts, send_lists, features.shape[0])
    for onehot, out in zip(sides, (first, second), strict=True):
        out[...] = dot(onehot, features[...], FIRST).astype(BF16)


def layer_kernel(
    rows, cols, tiles_hbm, own_hbm, halo_hbm, weight, labels,
    weight_out, grads,
    tiles, columns, sums, sems,
):
    count, tile = tiles.shape[0], tiles.shape[1]
    classes, hidden = weight.shape
    padded = grads.shape[1]
    nodes = labels.shape[1]
    group = 4
    copies = [
        pltpu.make_async_copy(own_hbm, columns.at[:, 0:2], sems.at[0]),
        pltpu.make_async_copy(halo_hbm, columns.at[:, 2:3], sems.at[1]),
        pltpu.make_async_copy(tiles_hbm, tiles, sems.at[2]),
    ]
    for copy in copies:
        copy.start()

    def masked(t):
        block = tiles[t]
        none = jnp.zeros_like(block)
        first = rows[t] == 0
        return jnp.where(first, block, none), jnp.where(first, none, block)

    def column(t):
        member = cols[t] // 3
        return columns[member, cols[t] - 3 * member]

    sums[...] = jnp.zeros_like(sums)
    grads[...] = jnp.zeros_like(grads)
    for copy in copies:
        copy.wait()
    for start in range(0, count, group):
        picks = [masked(t) for t in range(start, start + group)]
        left = jnp.concatenate(
            [jnp.concatenate([p[i] for p in picks], axis=1) for i in range(2)], axis=0
        )
        right = jnp.concatenate([column(t) for t in range(start, start + group)], axis=0)
        sums[...] += dot(left, right)

    total = sums[...]
    high = total.astype(BF16)
    low = (total - high.astype(F32)).astype(BF16)
    wide = jnp.concatenate(
        [weight[...].astype(F32), jnp.zeros((padded - classes, hidden), F32)], axis=0
    ).astype(BF16)
    logits = dot(wide, high, LAST) + dot(wide, low, LAST)
    kind = lax.broadcasted_iota(jnp.int32, (padded, nodes), 0)
    logits = jnp.where(kind < classes, logits, -jnp.inf)
    shifted = logits - jnp.max(logits, axis=0, keepdims=True)
    logp = shifted - jnp.log(jnp.sum(jnp.exp(shifted), axis=0, keepdims=True))
    onehot = kind == labels[...]
    losses = -jnp.sum(jnp.where(onehot, logp, 0.0), axis=0, keepdims=True)
    grad = (jnp.exp(logp) - onehot.astype(F32)).astype(BF16)

    weight_grad = dot(grad, high) + dot(grad, low)
    weight_grad = jnp.where(kind == classes, losses, weight_grad)
    weight_grad = weight_grad.astype(BF16)
    pieces = padded // PIECE
    weight_out[2 * pieces :] = jnp.zeros_like(weight_out[2 * pieces :])
    for i in range(2 * pieces):
        row, lane = i % pieces * PIECE, i // pieces * LANES
        weight_out[i] = weight_grad[row : row + PIECE, lane : lane + LANES]

    for start in range(0, count, 2):
        a, b = masked(start), masked(start + 1)
        right = jnp.concatenate([jnp.concatenate([a[i], b[i]], axis=1) for i in range(2)], axis=0)
        both = dot(grad, right)
        grads[cols[start]] += both[:, :tile]
        grads[cols[start + 1]] += both[:, tile:]

def sum_kernel(parts, out):
    summed = jnp.sum(parts[...].astype(F32), axis=0, keepdims=True)
    out[...] = jnp.broadcast_to(summed.astype(out.dtype), out.shape)


def rows_kernel(counts, send_lists, own, before, after, weight, out):
    padded = before.shape[0]
    classes = weight.shape[0]
    first, second = slots_onehot(counts, send_lists, out.shape[0])
    send = send_lists.shape[1]
    total = jnp.concatenate([own[0], own[1]], axis=1)
    total += dot(before[:, send:], first, LAST)
    total += dot(after[:, :send], second, LAST)
    grad = total[:classes].astype(BF16)
    out[...] = dot(grad, weight[...], FIRST).astype(BF16)


def last_kernel(scale, parts, weight_grad, loss):
    classes = weight_grad.shape[0]
    pieces = round_up(classes + 1, PIECE) // PIECE
    gathered = jnp.concatenate(
        [
            jnp.concatenate([parts[pieces * h + q].astype(F32) for q in range(pieces)], axis=0)
            for h in range(2)
        ],
        axis=1,
    )
    weight_grad[...] = gathered[:classes] * scale
    loss[...] = jnp.sum(gathered[classes : classes + 1], axis=1, keepdims=True) * scale


def per_device(features, weight, tiles, tile_rows, tile_cols, send_lists, counts, labels):
    nodes, hidden = features.shape
    classes = weight.shape[1]
    send = send_lists.shape[1]
    count, tile = tiles.shape[0], tiles.shape[1]
    reps = lax.axis_size("x")
    dom = AXES[:-1]
    domains = lax.axis_size(dom)
    near = ("zl", "y", "c")
    far = ("zh", "x")
    padded = round_up(classes + 1, PIECE)
    up = [(i, i + 1) for i in range(domains - 1)]
    down = [(i + 1, i) for i in range(domains - 1)]
    shape = jax.ShapeDtypeStruct
    weight = weight.T

    first, second = pl.pallas_call(
        pick_kernel,
        out_shape=(shape((send, hidden), BF16),) * 2,
        in_specs=[smem(), vmem(), vmem()],
        out_specs=(vmem(),) * 2,
    )(counts, send_lists, features)
    from_before = lax.ppermute(second, dom, up)
    from_after = lax.ppermute(first, dom, down)
    own_rows = lax.all_gather(features, "x", axis=0, tiled=True)
    halo_rows = lax.all_gather(
        jnp.concatenate([from_before, from_after], axis=0), "x", axis=0, tiled=True
    )

    weight_parts, parts = pl.pallas_call(
        layer_kernel,
        out_shape=(
            shape((lax.axis_size(near), PIECE, LANES), BF16),
            shape((3 * reps, padded, tile), F32),
        ),
        in_specs=[smem(), smem(), hbm(), hbm(), hbm(), vmem(), vmem()],
        out_specs=(vmem(),) * 2,
        scratch_shapes=[
            pltpu.VMEM((count, tile, tile), BF16),
            pltpu.VMEM((reps, 3, tile, hidden), BF16),
            pltpu.VMEM((nodes, hidden), F32),
            pltpu.SemaphoreType.DMA((3,)),
        ],
        compiler_params=params(56),
    )(
        tile_rows,
        tile_cols,
        tiles,
        own_rows.reshape(reps, 2, tile, hidden),
        halo_rows.reshape(reps, 1, tile, hidden),
        weight,
        labels.reshape(1, nodes),
    )

    def fold(parts, copies):
        return pl.pallas_call(
            sum_kernel,
            out_shape=shape((copies, *parts.shape[1:]), BF16),
            in_specs=[vmem()],
            out_specs=vmem(),
            compiler_params=params(4),
        )(parts)

    own = lax.psum_scatter(parts, "x", scatter_dimension=0, tiled=True)
    weight_parts = lax.all_to_all(weight_parts, near, 0, 0, tiled=True)
    weight_parts = fold(weight_parts, lax.axis_size(far))
    weight_parts = lax.all_to_all(weight_parts, far, 0, 0, tiled=True)
    weight_parts = fold(weight_parts, lax.axis_size(near))
    weight_parts = lax.all_to_all(weight_parts, near, 0, 0, tiled=True)

    halo = own[2].astype(BF16)
    before = lax.ppermute(halo, dom, up)
    after = lax.ppermute(halo, dom, down)
    grad_features = pl.pallas_call(
        rows_kernel,
        out_shape=shape((nodes, hidden), BF16),
        in_specs=[smem()] + [vmem()] * 5,
        out_specs=vmem(),
        compiler_params=params(4),
    )(counts, send_lists, own, before, after, weight)

    scale = 1.0 / (domains * reps * nodes)
    weight_grad, loss = pl.pallas_call(
        lambda *refs: last_kernel(scale, *refs),
        out_shape=(shape((classes, hidden), F32), shape((1, 1), F32)),
        in_specs=[vmem()],
        out_specs=(vmem(),) * 2,
        compiler_params=params(4),
    )(weight_parts)
    return grad_features, weight_grad.T, loss.reshape(())


def solution(mesh):
    split = Mesh(mesh.devices.reshape(SHAPE), AXES)
    both = AXES
    placed = (
        P(both, None),
        P(),
        P(both, None, None),
        P(both),
        P(both),
        P(both, None),
        P(both),
        P(both),
    )
    return jax.shard_map(
        per_device,
        mesh=split,
        in_specs=placed,
        out_specs=(P(both, None), P(), P()),
        check_vma=False,
    )
```

```python
import jax
import jax.numpy as jnp
from jax import lax
from jax.experimental import pallas as pl
from jax.experimental.pallas import tpu as pltpu
from jax.sharding import Mesh, PartitionSpec as P

F32 = jnp.float32
BF16 = jnp.bfloat16
LANES = 128
PIECE = 16
EARLY = 192
SHAPE = (4, 2, 8, 2, 8)
AXES = ("zh", "zl", "y", "c", "x")
LAST = (((1,), (1,)), ((), ()))
FIRST = (((0,), (0,)), ((), ()))
PLAIN = (((1,), (0,)), ((), ()))


def round_up(value, unit):
    return -(-value // unit) * unit


def dot(a, b, dims=PLAIN):
    return lax.dot_general(a, b, dims, preferred_element_type=F32)


def vmem():
    return pl.BlockSpec(memory_space=pltpu.VMEM)


def smem():
    return pl.BlockSpec(memory_space=pltpu.SMEM)


def hbm():
    return pl.BlockSpec(memory_space=pl.ANY)


def params(mib):
    return pltpu.CompilerParams(vmem_limit_bytes=mib * 2**20)


def slots_onehot(counts, send_lists, rows):
    send = send_lists.shape[1]
    row = lax.broadcasted_iota(jnp.int32, (rows, send), 0)
    slot = lax.broadcasted_iota(jnp.int32, (rows, send), 1)
    sides = [
        jnp.where((row == send_lists[i : i + 1, :]) & (slot < counts[i]), 1.0, 0.0)
        for i in range(2)
    ]
    return [side.astype(BF16) for side in sides]


def pick_kernel(counts, send_lists, features, first, second):
    sides = slots_onehot(counts, send_lists, features.shape[0])
    for onehot, out in zip(sides, (first, second), strict=True):
        out[...] = dot(onehot, features[...], FIRST).astype(BF16)


def layer_kernel(
    rows, cols, tiles_hbm, own_hbm, rest_hbm, weight, labels,
    weight_out, out,
    tiles, columns, sums, grads, sems,
):
    count, tile = tiles.shape[0], tiles.shape[1]
    classes, hidden = weight.shape
    padded = grads.shape[1]
    nodes = labels.shape[1]
    early = own_hbm.shape[1]
    group = 4
    copies = [
        pltpu.make_async_copy(own_hbm, columns.at[:, :early], sems.at[0]),
        pltpu.make_async_copy(rest_hbm, columns.at[:, early:], sems.at[1]),
        pltpu.make_async_copy(tiles_hbm, tiles, sems.at[2]),
    ]
    for copy in copies:
        copy.start()

    def masked(t):
        block = tiles[t]
        none = jnp.zeros_like(block)
        first = rows[t] == 0
        return jnp.where(first, block, none), jnp.where(first, none, block)

    def column(t):
        member = cols[t] // 3
        start = pl.multiple_of((cols[t] - 3 * member) * tile, tile)
        return columns[member, pl.ds(start, tile), :]

    sums[...] = jnp.zeros_like(sums)
    grads[...] = jnp.zeros_like(grads)
    for copy in copies:
        copy.wait()
    for start in range(0, count, group):
        picks = [masked(t) for t in range(start, start + group)]
        left = jnp.concatenate(
            [jnp.concatenate([p[i] for p in picks], axis=1) for i in range(2)], axis=0
        )
        right = jnp.concatenate([column(t) for t in range(start, start + group)], axis=0)
        sums[...] += dot(left, right)

    total = sums[...]
    high = total.astype(BF16)
    low = (total - high.astype(F32)).astype(BF16)
    wide = jnp.concatenate(
        [weight[...].astype(F32), jnp.zeros((padded - classes, hidden), F32)], axis=0
    ).astype(BF16)
    logits = dot(wide, high, LAST) + dot(wide, low, LAST)
    kind = lax.broadcasted_iota(jnp.int32, (padded, nodes), 0)
    logits = jnp.where(kind < classes, logits, -jnp.inf)
    shifted = logits - jnp.max(logits, axis=0, keepdims=True)
    logp = shifted - jnp.log(jnp.sum(jnp.exp(shifted), axis=0, keepdims=True))
    onehot = kind == labels[...]
    losses = -jnp.sum(jnp.where(onehot, logp, 0.0), axis=0, keepdims=True)
    grad = (jnp.exp(logp) - onehot.astype(F32)).astype(BF16)

    weight_grad = dot(grad, high) + dot(grad, low)
    weight_grad = jnp.where(kind == classes, losses, weight_grad)
    weight_grad = weight_grad.astype(BF16)
    pieces = padded // PIECE
    weight_out[2 * pieces :] = jnp.zeros_like(weight_out[2 * pieces :])
    for i in range(2 * pieces):
        row, lane = i % pieces * PIECE, i // pieces * LANES
        weight_out[i] = weight_grad[row : row + PIECE, lane : lane + LANES]

    for start in range(0, count, 2):
        a, b = masked(start), masked(start + 1)
        right = jnp.concatenate([jnp.concatenate([a[i], b[i]], axis=1) for i in range(2)], axis=0)
        both = dot(grad, right)
        grads[cols[start]] += both[:, :tile]
        grads[cols[start + 1]] += both[:, tile:]
    for r in range(out.shape[0]):
        for j in range(3):
            out[r, j * padded : (j + 1) * padded, :] = grads[3 * r + j].astype(BF16)


def layer_scratch(reps, nodes, hidden, count, tile, padded):
    return [
        pltpu.VMEM((count, tile, tile), BF16),
        pltpu.VMEM((reps, 3 * tile, hidden), BF16),
        pltpu.VMEM((nodes, hidden), F32),
        pltpu.VMEM((3 * reps, padded, tile), F32),
        pltpu.SemaphoreType.DMA((3,)),
    ]


def fold_kernel(parts, own, halo):
    padded = halo.shape[0]
    summed = jnp.sum(parts[...].astype(F32), axis=0)
    own[...] = summed[: 2 * padded]
    halo[...] = summed[2 * padded :].astype(BF16)

def sum_kernel(parts, out):
    out[...] = jnp.sum(parts[...].astype(F32), axis=0)


def rows_kernel(counts, send_lists, own, before, after, weight, out):
    padded = before.shape[0]
    classes = weight.shape[0]
    first, second = slots_onehot(counts, send_lists, out.shape[0])
    send = send_lists.shape[1]
    total = jnp.concatenate([own[:padded], own[padded:]], axis=1)
    total += dot(before[:, send:], first, LAST)
    total += dot(after[:, :send], second, LAST)
    grad = total[:classes].astype(BF16)
    out[...] = dot(grad, weight[...], FIRST).astype(BF16)


def last_kernel(scale, parts, weight_grad, loss):
    classes = weight_grad.shape[0]
    pieces = round_up(classes + 1, PIECE) // PIECE
    gathered = jnp.concatenate(
        [
            jnp.concatenate([parts[pieces * h + q].astype(F32) for q in range(pieces)], axis=0)
            for h in range(2)
        ],
        axis=1,
    )
    weight_grad[...] = gathered[:classes] * scale
    loss[...] = jnp.sum(gathered[classes : classes + 1], axis=1, keepdims=True) * scale


def per_device(features, weight, tiles, tile_rows, tile_cols, send_lists, counts, labels):
    nodes, hidden = features.shape
    classes = weight.shape[1]
    send = send_lists.shape[1]
    count, tile = tiles.shape[0], tiles.shape[1]
    reps = lax.axis_size("x")
    dom = AXES[:-1]
    domains = lax.axis_size(dom)
    near = ("zl", "c", "x")
    padded = round_up(classes + 1, PIECE)
    up = [(i, i + 1) for i in range(domains - 1)]
    down = [(i + 1, i) for i in range(domains - 1)]
    shape = jax.ShapeDtypeStruct
    weight = weight.T

    first, second = pl.pallas_call(
        pick_kernel,
        out_shape=(shape((send, hidden), BF16),) * 2,
        in_specs=[smem(), vmem(), vmem()],
        out_specs=(vmem(),) * 2,
    )(counts, send_lists, features)
    from_before = lax.ppermute(second, dom, up)
    from_after = lax.ppermute(first, dom, down)
    own_rows = lax.all_to_all(
        jnp.broadcast_to(features[:EARLY][None], (reps, EARLY, hidden)), "x", 0, 0, tiled=True
    )
    rest = jnp.concatenate([features[EARLY:], from_before, from_after], axis=0)
    rest_rows = lax.all_gather(rest, "x", axis=0)

    weight_parts, parts = pl.pallas_call(
        layer_kernel,
        out_shape=(
            shape((lax.axis_size(near), PIECE, LANES), BF16),
            shape((reps, 3 * padded, LANES), BF16),
        ),
        in_specs=[smem(), smem(), hbm(), hbm(), hbm(), vmem(), vmem()],
        out_specs=(vmem(),) * 2,
        scratch_shapes=layer_scratch(reps, nodes, hidden, count, tile, padded),
        compiler_params=params(56),
    )(tile_rows, tile_cols, tiles, own_rows, rest_rows, weight, labels.reshape(1, nodes))

    weight_parts = lax.all_to_all(weight_parts, near, 0, 0, tiled=True)
    weight_part = pl.pallas_call(
        sum_kernel,
        out_shape=shape(weight_parts.shape[1:], F32),
        in_specs=[vmem()],
        out_specs=vmem(),
        compiler_params=params(4),
    )(weight_parts)
    weight_part, parts = lax.optimization_barrier((weight_part, parts))
    parts = lax.all_to_all(parts, "x", 0, 0, tiled=True)
    weight_part = lax.psum(lax.psum(weight_part, "y"), "zh").astype(BF16)
    copies = jnp.broadcast_to(weight_part[None], weight_parts.shape)
    weight_parts = lax.all_to_all(copies, near, 0, 0, tiled=True)

    own, halo = pl.pallas_call(
        fold_kernel,
        out_shape=(shape((2 * padded, LANES), F32), shape((padded, LANES), BF16)),
        in_specs=[vmem()],
        out_specs=(vmem(),) * 2,
        compiler_params=params(8),
    )(parts)
    before = lax.ppermute(halo, dom, up)
    after = lax.ppermute(halo, dom, down)
    grad_features = pl.pallas_call(
        rows_kernel,
        out_shape=shape((nodes, hidden), BF16),
        in_specs=[smem()] + [vmem()] * 5,
        out_specs=vmem(),
        compiler_params=params(4),
    )(counts, send_lists, own, before, after, weight)

    scale = 1.0 / (domains * reps * nodes)
    weight_grad, loss = pl.pallas_call(
        lambda *refs: last_kernel(scale, *refs),
        out_shape=(shape((classes, hidden), F32), shape((1, 1), F32)),
        in_specs=[vmem()],
        out_specs=(vmem(),) * 2,
        compiler_params=params(4),
    )(weight_parts)
    return grad_features, weight_grad.T, loss.reshape(())


def solution(mesh):
    split = Mesh(mesh.devices.reshape(SHAPE), AXES)
    both = AXES
    placed = (
        P(both, None),
        P(),
        P(both, None, None),
        P(both),
        P(both),
        P(both, None),
        P(both),
        P(both),
    )
    return jax.shard_map(
        per_device,
        mesh=split,
        in_specs=placed,
        out_specs=(P(both, None), P(), P()),
        check_vma=False,
    )
```

```python
import jax
import jax.numpy as jnp
from jax import lax
from jax.experimental import pallas as pl
from jax.experimental.pallas import tpu as pltpu
from jax.sharding import Mesh, PartitionSpec as P

F32 = jnp.float32
BF16 = jnp.bfloat16
LANES = 128
PIECE = 16
SHAPE = (4, 2, 8, 2, 8)
AXES = ("zh", "zl", "y", "c", "x")
NEAR = ("zl", "y", "c")
FAR = ("zh", "x")
CHUNK = 16
LAST = (((1,), (1,)), ((), ()))
FIRST = (((0,), (0,)), ((), ()))
PLAIN = (((1,), (0,)), ((), ()))


def round_up(value, unit):
    return -(-value // unit) * unit


def dot(a, b, dims=PLAIN):
    return lax.dot_general(a, b, dims, preferred_element_type=F32)


def vmem():
    return pl.BlockSpec(memory_space=pltpu.VMEM)


def smem():
    return pl.BlockSpec(memory_space=pltpu.SMEM)


def hbm():
    return pl.BlockSpec(memory_space=pl.ANY)


def params(mib):
    return pltpu.CompilerParams(vmem_limit_bytes=mib * 2**20)


def slots_onehot(counts, send_lists, rows):
    send = send_lists.shape[1]
    row = lax.broadcasted_iota(jnp.int32, (rows, send), 0)
    slot = lax.broadcasted_iota(jnp.int32, (rows, send), 1)
    sides = [
        jnp.where((row == send_lists[i : i + 1, :]) & (slot < counts[i]), 1.0, 0.0)
        for i in range(2)
    ]
    return [side.astype(BF16) for side in sides]


def pick_kernel(core, counts, send_lists, features, partner, outside):
    first, second = slots_onehot(counts, send_lists, features.shape[0])
    even = core[0] == 0
    partner[...] = dot(jnp.where(even, second, first), features[...], FIRST).astype(BF16)
    outside[...] = dot(jnp.where(even, first, second), features[...], FIRST).astype(BF16)


def layer_kernel(
    core, rows, cols, tiles_hbm, own_hbm, halo_hbm, weight, labels,
    weight_out, grads,
    tiles, columns, sums, sems,
):
    count, tile = tiles.shape[0], tiles.shape[1]
    classes, hidden = weight.shape
    padded = grads.shape[1]
    nodes = labels.shape[1]
    send = tile // 2
    partner_at = pl.multiple_of(send * (1 - core[0]), send)
    outside_at = pl.multiple_of(send * core[0], send)
    copies = [
        pltpu.make_async_copy(own_hbm, columns.at[:, 0:2], sems.at[0]),
        pltpu.make_async_copy(
            halo_hbm.at[:, :send], columns.at[:, 2, pl.ds(partner_at, send)], sems.at[1]
        ),
        pltpu.make_async_copy(
            halo_hbm.at[:, send:], columns.at[:, 2, pl.ds(outside_at, send)], sems.at[2]
        ),
    ]
    tile_copies = [
        pltpu.make_async_copy(
            tiles_hbm.at[pl.ds(start, CHUNK)],
            tiles.at[pl.ds(start, CHUNK)],
            sems.at[3 + start // CHUNK],
        )
        for start in range(0, count, CHUNK)
    ]
    for copy in copies + tile_copies:
        copy.start()

    def masked(t):
        block = tiles[t]
        none = jnp.zeros_like(block)
        first = rows[t] == 0
        return jnp.where(first, block, none), jnp.where(first, none, block)

    def column(t):
        member = cols[t] // 3
        return columns[member, cols[t] - 3 * member]

    sums[...] = jnp.zeros_like(sums)
    grads[...] = jnp.zeros_like(grads)
    for copy in copies:
        copy.wait()
    for t in range(count):
        if t % CHUNK == 0:
            tile_copies[t // CHUNK].wait()
        at = pl.ds(pl.multiple_of(rows[t] * tile, tile), tile)
        sums[at, :] += dot(tiles[t], column(t))

    total = sums[...]
    high = total.astype(BF16)
    low = (total - high.astype(F32)).astype(BF16)
    wide = jnp.concatenate(
        [weight[...].astype(F32), jnp.zeros((padded - classes, hidden), F32)], axis=0
    ).astype(BF16)
    logits = dot(wide, high, LAST) + dot(wide, low, LAST)
    kind = lax.broadcasted_iota(jnp.int32, (padded, nodes), 0)
    logits = jnp.where(kind < classes, logits, -jnp.inf)
    shifted = logits - jnp.max(logits, axis=0, keepdims=True)
    logp = shifted - jnp.log(jnp.sum(jnp.exp(shifted), axis=0, keepdims=True))
    onehot = kind == labels[...]
    losses = -jnp.sum(jnp.where(onehot, logp, 0.0), axis=0, keepdims=True)
    grad = (jnp.exp(logp) - onehot.astype(F32)).astype(BF16)

    weight_grad = dot(grad, high) + dot(grad, low)
    weight_grad = jnp.where(kind == classes, losses, weight_grad)
    weight_grad = weight_grad.astype(BF16)
    pieces = padded // PIECE
    weight_out[2 * pieces :] = jnp.zeros_like(weight_out[2 * pieces :])
    for i in range(2 * pieces):
        row, lane = i % pieces * PIECE, i // pieces * LANES
        weight_out[i] = weight_grad[row : row + PIECE, lane : lane + LANES]

    for start in range(0, count, 2):
        a, b = masked(start), masked(start + 1)
        right = jnp.concatenate([jnp.concatenate([a[i], b[i]], axis=1) for i in range(2)], axis=0)
        both = dot(grad, right)
        grads[cols[start]] += both[:, :tile]
        grads[cols[start + 1]] += both[:, tile:]


def sum_kernel(parts, out):
    summed = jnp.sum(parts[...].astype(F32), axis=0, keepdims=True)
    out[...] = jnp.broadcast_to(summed.astype(out.dtype), out.shape)


def rows_kernel(core, counts, send_lists, own, partner, outside, weight, out):
    padded = partner.shape[0]
    even = core[0] == 0
    before = jnp.where(even, outside[...], partner[...])
    after = jnp.where(even, partner[...], outside[...])
    classes = weight.shape[0]
    first, second = slots_onehot(counts, send_lists, out.shape[0])
    send = send_lists.shape[1]
    total = jnp.concatenate([own[0], own[1]], axis=1)
    total += dot(before[:, send:], first, LAST)
    total += dot(after[:, :send], second, LAST)
    grad = total[:classes].astype(BF16)
    out[...] = dot(grad, weight[...], FIRST).astype(BF16)


def last_kernel(scale, parts, weight_grad, loss):
    classes = weight_grad.shape[0]
    pieces = round_up(classes + 1, PIECE) // PIECE
    gathered = jnp.concatenate(
        [
            jnp.concatenate([parts[pieces * h + q].astype(F32) for q in range(pieces)], axis=0)
            for h in range(2)
        ],
        axis=1,
    )
    weight_grad[...] = gathered[:classes] * scale
    loss[...] = jnp.sum(gathered[classes : classes + 1], axis=1, keepdims=True) * scale


def per_device(features, weight, tiles, tile_rows, tile_cols, send_lists, counts, labels):
    nodes, hidden = features.shape
    classes = weight.shape[1]
    send = send_lists.shape[1]
    count, tile = tiles.shape[0], tiles.shape[1]
    reps = lax.axis_size("x")
    dom = AXES[:-1]
    domains = lax.axis_size(dom)
    padded = round_up(classes + 1, PIECE)
    core = jnp.reshape(lax.axis_index("c"), (1,)).astype(jnp.int32)
    outer = [(i, i + 1) for i in range(1, domains - 1, 2)]
    outer += [(target, source) for source, target in outer]

    def exchange(to_partner, to_outside):
        return (
            lax.ppermute(to_partner, "c", [(0, 1), (1, 0)]),
            lax.ppermute(to_outside, dom, outer),
        )

    shape = jax.ShapeDtypeStruct
    weight = weight.T

    picked = pl.pallas_call(
        pick_kernel,
        out_shape=(shape((send, hidden), BF16),) * 2,
        in_specs=[smem(), smem(), vmem(), vmem()],
        out_specs=(vmem(),) * 2,
    )(core, counts, send_lists, features)
    halo = jnp.concatenate(exchange(*picked), axis=0)
    own_rows = lax.all_gather(features, "x", axis=0, tiled=True)
    halo_rows = lax.all_gather(halo, "x", axis=0)

    weight_parts, parts = pl.pallas_call(
        layer_kernel,
        out_shape=(
            shape((lax.axis_size(NEAR), PIECE, LANES), BF16),
            shape((3 * reps, padded, tile), F32),
        ),
        in_specs=[smem(), smem(), smem(), hbm(), hbm(), hbm(), vmem(), vmem()],
        out_specs=(vmem(),) * 2,
        scratch_shapes=[
            pltpu.VMEM((count, tile, tile), BF16),
            pltpu.VMEM((reps, 3, tile, hidden), BF16),
            pltpu.VMEM((nodes, hidden), F32),
            pltpu.SemaphoreType.DMA((3 + count // CHUNK,)),
        ],
        compiler_params=params(56),
    )(
        core,
        tile_rows,
        tile_cols,
        tiles,
        own_rows.reshape(reps, 2, tile, hidden),
        halo_rows,
        weight,
        labels.reshape(1, nodes),
    )

    def fold(parts, copies):
        return pl.pallas_call(
            sum_kernel,
            out_shape=shape((copies, *parts.shape[1:]), BF16),
            in_specs=[vmem()],
            out_specs=vmem(),
            compiler_params=params(4),
        )(parts)

    own = lax.psum_scatter(parts, "x", scatter_dimension=0, tiled=True)
    weight_parts = lax.all_to_all(weight_parts, NEAR, 0, 0, tiled=True)
    weight_parts = fold(weight_parts, lax.axis_size(FAR))
    weight_parts = lax.all_to_all(weight_parts, FAR, 0, 0, tiled=True)
    weight_parts = fold(weight_parts, lax.axis_size(NEAR))
    weight_parts = lax.all_to_all(weight_parts, NEAR, 0, 0, tiled=True)

    halo = own[2].astype(BF16)
    grad_features = pl.pallas_call(
        rows_kernel,
        out_shape=shape((nodes, hidden), BF16),
        in_specs=[smem(), smem()] + [vmem()] * 5,
        out_specs=vmem(),
        compiler_params=params(4),
    )(core, counts, send_lists, own, *exchange(halo, halo), weight)
    weight_parts, grad_features = lax.optimization_barrier((weight_parts, grad_features))

    scale = 1.0 / (domains * reps * nodes)
    weight_grad, loss = pl.pallas_call(
        lambda *refs: last_kernel(scale, *refs),
        out_shape=(shape((classes, hidden), F32), shape((1, 1), F32)),
        in_specs=[vmem()],
        out_specs=(vmem(),) * 2,
        compiler_params=params(4),
    )(weight_parts)
    return grad_features, weight_grad.T, loss.reshape(())


def solution(mesh):
    split = Mesh(mesh.devices.reshape(SHAPE), AXES)
    both = AXES
    placed = (
        P(both, None),
        P(),
        P(both, None, None),
        P(both),
        P(both),
        P(both, None),
        P(both),
        P(both),
    )
    return jax.shard_map(
        per_device,
        mesh=split,
        in_specs=placed,
        out_specs=(P(both, None), P(), P()),
        check_vma=False,
    )
```

```python
import jax
import jax.numpy as jnp
from jax import lax
from jax.experimental import pallas as pl
from jax.experimental.pallas import tpu as pltpu
from jax.sharding import Mesh, PartitionSpec as P

F32 = jnp.float32
BF16 = jnp.bfloat16
LANES = 128
PIECE = 16
EARLY = 192
SHAPE = (4, 2, 8, 2, 8)
AXES = ("zh", "zl", "y", "c", "x")
NEAR = ("zl", "c", "x")
FAR = ("y", "zh")
CHUNK = 16
LIMIT = 56
LAST = (((1,), (1,)), ((), ()))
FIRST = (((0,), (0,)), ((), ()))
PLAIN = (((1,), (0,)), ((), ()))


def round_up(value, unit):
    return -(-value // unit) * unit


def dot(a, b, dims=PLAIN):
    return lax.dot_general(a, b, dims, preferred_element_type=F32)


def vmem():
    return pl.BlockSpec(memory_space=pltpu.VMEM)


def smem():
    return pl.BlockSpec(memory_space=pltpu.SMEM)


def hbm():
    return pl.BlockSpec(memory_space=pl.ANY)


def params(mib):
    return pltpu.CompilerParams(vmem_limit_bytes=mib * 2**20)


def slots_onehot(counts, send_lists, rows):
    send = send_lists.shape[1]
    row = lax.broadcasted_iota(jnp.int32, (rows, send), 0)
    slot = lax.broadcasted_iota(jnp.int32, (rows, send), 1)
    sides = [
        jnp.where((row == send_lists[i : i + 1, :]) & (slot < counts[i]), 1.0, 0.0)
        for i in range(2)
    ]
    return [side.astype(BF16) for side in sides]


def pick_kernel(core, counts, send_lists, features, partner, outside, copies):
    copies[...] = jnp.broadcast_to(features[: copies.shape[1]][None], copies.shape)
    first, second = slots_onehot(counts, send_lists, features.shape[0])
    even = core[0] == 0
    partner[...] = dot(jnp.where(even, second, first), features[...], FIRST).astype(BF16)
    outside[...] = dot(jnp.where(even, first, second), features[...], FIRST).astype(BF16)


def layer_kernel(
    core, rows, cols, tiles_hbm, own_hbm, rest_hbm, weight, labels,
    weight_out, out,
    tiles, columns, sums, grads, sems,
):
    count, tile = tiles.shape[0], tiles.shape[1]
    classes, hidden = weight.shape
    padded = grads.shape[1]
    nodes = labels.shape[1]
    send, early = tile // 2, own_hbm.shape[1]
    late = nodes - early
    partner_at = pl.multiple_of(nodes + send * (1 - core[0]), send)
    outside_at = pl.multiple_of(nodes + send * core[0], send)
    copies = [
        pltpu.make_async_copy(own_hbm, columns.at[:, :early], sems.at[0]),
        pltpu.make_async_copy(rest_hbm.at[:, :late], columns.at[:, early:nodes], sems.at[1]),
        pltpu.make_async_copy(
            rest_hbm.at[:, late : late + send], columns.at[:, pl.ds(partner_at, send)], sems.at[2]
        ),
        pltpu.make_async_copy(
            rest_hbm.at[:, late + send :], columns.at[:, pl.ds(outside_at, send)], sems.at[3]
        ),
    ]
    tile_copies = [
        pltpu.make_async_copy(
            tiles_hbm.at[pl.ds(start, CHUNK)],
            tiles.at[pl.ds(start, CHUNK)],
            sems.at[4 + start // CHUNK],
        )
        for start in range(0, count, CHUNK)
    ]
    for copy in copies + tile_copies:
        copy.start()

    def masked(t):
        block = tiles[t]
        none = jnp.zeros_like(block)
        first = rows[t] == 0
        return jnp.where(first, block, none), jnp.where(first, none, block)

    def column(t):
        member = cols[t] // 3
        start = pl.multiple_of((cols[t] - 3 * member) * tile, tile)
        return columns[member, pl.ds(start, tile), :]

    sums[...] = jnp.zeros_like(sums)
    grads[...] = jnp.zeros_like(grads)
    for copy in copies:
        copy.wait()
    for t in range(count):
        if t % CHUNK == 0:
            tile_copies[t // CHUNK].wait()
        at = pl.ds(pl.multiple_of(rows[t] * tile, tile), tile)
        sums[at, :] += dot(tiles[t], column(t))

    total = sums[...]
    high = total.astype(BF16)
    low = (total - high.astype(F32)).astype(BF16)
    wide = jnp.concatenate(
        [weight[...].astype(F32), jnp.zeros((padded - classes, hidden), F32)], axis=0
    ).astype(BF16)
    logits = dot(wide, high, LAST) + dot(wide, low, LAST)
    kind = lax.broadcasted_iota(jnp.int32, (padded, nodes), 0)
    logits = jnp.where(kind < classes, logits, -jnp.inf)
    shifted = logits - jnp.max(logits, axis=0, keepdims=True)
    logp = shifted - jnp.log(jnp.sum(jnp.exp(shifted), axis=0, keepdims=True))
    onehot = kind == labels[...]
    losses = -jnp.sum(jnp.where(onehot, logp, 0.0), axis=0, keepdims=True)
    grad = (jnp.exp(logp) - onehot.astype(F32)).astype(BF16)

    weight_grad = dot(grad, high) + dot(grad, low)
    weight_grad = jnp.where(kind == classes, losses, weight_grad)
    weight_grad = weight_grad.astype(BF16)
    pieces = padded // PIECE
    weight_out[2 * pieces :] = jnp.zeros_like(weight_out[2 * pieces :])
    for i in range(2 * pieces):
        row, lane = i % pieces * PIECE, i // pieces * LANES
        weight_out[i] = weight_grad[row : row + PIECE, lane : lane + LANES]

    for start in range(0, count, 2):
        a, b = masked(start), masked(start + 1)
        right = jnp.concatenate([jnp.concatenate([a[i], b[i]], axis=1) for i in range(2)], axis=0)
        both = dot(grad, right)
        grads[cols[start]] += both[:, :tile]
        grads[cols[start + 1]] += both[:, tile:]
    for r in range(out.shape[0]):
        for j in range(3):
            out[r, j * padded : (j + 1) * padded, :] = grads[3 * r + j].astype(BF16)


def fold_kernel(parts, own, halo):
    padded = halo.shape[0]
    summed = jnp.sum(parts[...].astype(F32), axis=0)
    own[...] = summed[: 2 * padded]
    halo[...] = summed[2 * padded :].astype(BF16)

def sum_kernel(parts, out):
    out[...] = jnp.sum(parts[...].astype(F32), axis=0)


def rows_kernel(core, counts, send_lists, own, partner, outside, weight, out):
    padded = partner.shape[0]
    even = core[0] == 0
    before = jnp.where(even, outside[...], partner[...])
    after = jnp.where(even, partner[...], outside[...])
    classes = weight.shape[0]
    first, second = slots_onehot(counts, send_lists, out.shape[0])
    send = send_lists.shape[1]
    total = jnp.concatenate([own[:padded], own[padded:]], axis=1)
    total += dot(before[:, send:], first, LAST)
    total += dot(after[:, :send], second, LAST)
    grad = total[:classes].astype(BF16)
    out[...] = dot(grad, weight[...], FIRST).astype(BF16)


def last_kernel(scale, parts, weight_grad, loss):
    classes = weight_grad.shape[0]
    pieces = round_up(classes + 1, PIECE) // PIECE
    gathered = jnp.concatenate(
        [
            jnp.concatenate([parts[pieces * h + q].astype(F32) for q in range(pieces)], axis=0)
            for h in range(2)
        ],
        axis=1,
    )
    weight_grad[...] = gathered[:classes] * scale
    loss[...] = jnp.sum(gathered[classes : classes + 1], axis=1, keepdims=True) * scale


def per_device(features, weight, tiles, tile_rows, tile_cols, send_lists, counts, labels):
    nodes, hidden = features.shape
    classes = weight.shape[1]
    send = send_lists.shape[1]
    count, tile = tiles.shape[0], tiles.shape[1]
    reps = lax.axis_size("x")
    dom = AXES[:-1]
    domains = lax.axis_size(dom)
    padded = round_up(classes + 1, PIECE)
    core = jnp.reshape(lax.axis_index("c"), (1,)).astype(jnp.int32)
    outer = [(i, i + 1) for i in range(1, domains - 1, 2)]
    outer += [(target, source) for source, target in outer]

    def exchange(to_partner, to_outside):
        return (
            lax.ppermute(to_partner, "c", [(0, 1), (1, 0)]),
            lax.ppermute(to_outside, dom, outer),
        )

    shape = jax.ShapeDtypeStruct
    weight = weight.T

    *picked, copies = pl.pallas_call(
        pick_kernel,
        out_shape=(
            shape((send, hidden), BF16),
            shape((send, hidden), BF16),
            shape((reps, EARLY, hidden), BF16),
        ),
        in_specs=[smem(), smem(), vmem(), vmem()],
        out_specs=(vmem(),) * 3,
    )(core, counts, send_lists, features)
    own_rows = lax.all_to_all(copies, "x", 0, 0, tiled=True)
    rest = jnp.concatenate([features[EARLY:], *exchange(*picked)], axis=0)
    rest_rows = lax.all_gather(rest, "x", axis=0)

    weight_parts, parts = pl.pallas_call(
        layer_kernel,
        out_shape=(
            shape((lax.axis_size(NEAR), PIECE, LANES), BF16),
            shape((reps, 3 * padded, LANES), BF16),
        ),
        in_specs=[smem(), smem(), smem(), hbm(), hbm(), hbm(), vmem(), vmem()],
        out_specs=(vmem(),) * 2,
        scratch_shapes=[
            pltpu.VMEM((count, tile, tile), BF16),
            pltpu.VMEM((reps, 3 * tile, hidden), BF16),
            pltpu.VMEM((nodes, hidden), F32),
            pltpu.VMEM((3 * reps, padded, tile), F32),
            pltpu.SemaphoreType.DMA((4 + count // CHUNK,)),
        ],
        compiler_params=params(LIMIT),
    )(core, tile_rows, tile_cols, tiles, own_rows, rest_rows, weight, labels.reshape(1, nodes))

    weight_parts = lax.all_to_all(weight_parts, NEAR, 0, 0, tiled=True)
    weight_part = pl.pallas_call(
        sum_kernel,
        out_shape=shape(weight_parts.shape[1:], F32),
        in_specs=[vmem()],
        out_specs=vmem(),
        compiler_params=params(4),
    )(weight_parts)
    weight_part, parts = lax.optimization_barrier((weight_part, parts))
    parts = lax.all_to_all(parts, "x", 0, 0, tiled=True)
    weight_part = lax.psum(lax.psum(weight_part, "y"), "zh").astype(BF16)
    copies = jnp.broadcast_to(weight_part[None], weight_parts.shape)
    weight_parts = lax.all_to_all(copies, NEAR, 0, 0, tiled=True)

    own, halo = pl.pallas_call(
        fold_kernel,
        out_shape=(shape((2 * padded, LANES), F32), shape((padded, LANES), BF16)),
        in_specs=[vmem()],
        out_specs=(vmem(),) * 2,
        compiler_params=params(8),
    )(parts)
    grad_features = pl.pallas_call(
        rows_kernel,
        out_shape=shape((nodes, hidden), BF16),
        in_specs=[smem(), smem()] + [vmem()] * 5,
        out_specs=vmem(),
        compiler_params=params(4),
    )(core, counts, send_lists, own, *exchange(halo, halo), weight)
    weight_parts, grad_features = lax.optimization_barrier((weight_parts, grad_features))

    scale = 1.0 / (domains * reps * nodes)
    weight_grad, loss = pl.pallas_call(
        lambda *refs: last_kernel(scale, *refs),
        out_shape=(shape((classes, hidden), F32), shape((1, 1), F32)),
        in_specs=[vmem()],
        out_specs=(vmem(),) * 2,
        compiler_params=params(4),
    )(weight_parts)
    return grad_features, weight_grad.T, loss.reshape(())


def solution(mesh):
    split = Mesh(mesh.devices.reshape(SHAPE), AXES)
    both = AXES
    placed = (
        P(both, None),
        P(),
        P(both, None, None),
        P(both),
        P(both),
        P(both, None),
        P(both),
        P(both),
    )
    return jax.shard_map(
        per_device,
        mesh=split,
        in_specs=placed,
        out_specs=(P(both, None), P(), P()),
        check_vma=False,
    )
```

```python
import jax
import jax.numpy as jnp
from jax import lax
from jax.experimental import pallas as pl
from jax.experimental.pallas import tpu as pltpu
from jax.sharding import Mesh, PartitionSpec as P

F32 = jnp.float32
BF16 = jnp.bfloat16
LANES = 128
PIECE = 16
SHAPE = (4, 2, 8, 2, 8)
AXES = ("zh", "zl", "y", "c", "x")
NEAR = ("zl", "y", "c")
FAR = ("zh", "x")
CHUNK = 16
LAST = (((1,), (1,)), ((), ()))
FIRST = (((0,), (0,)), ((), ()))
PLAIN = (((1,), (0,)), ((), ()))


def round_up(value, unit):
    return -(-value // unit) * unit


def dot(a, b, dims=PLAIN):
    return lax.dot_general(a, b, dims, preferred_element_type=F32)


def vmem():
    return pl.BlockSpec(memory_space=pltpu.VMEM)


def smem():
    return pl.BlockSpec(memory_space=pltpu.SMEM)


def hbm():
    return pl.BlockSpec(memory_space=pl.ANY)


def params(mib):
    return pltpu.CompilerParams(vmem_limit_bytes=mib * 2**20)


def slots_onehot(counts, send_lists, rows):
    send = send_lists.shape[1]
    row = lax.broadcasted_iota(jnp.int32, (rows, send), 0)
    slot = lax.broadcasted_iota(jnp.int32, (rows, send), 1)
    sides = [
        jnp.where((row == send_lists[i : i + 1, :]) & (slot < counts[i]), 1.0, 0.0)
        for i in range(2)
    ]
    return [side.astype(BF16) for side in sides]


def pick_kernel(core, counts, send_lists, features, partner, outside):
    first, second = slots_onehot(counts, send_lists, features.shape[0])
    even = core[0] == 0
    partner[...] = dot(jnp.where(even, second, first), features[...], FIRST).astype(BF16)
    outside[...] = dot(jnp.where(even, first, second), features[...], FIRST).astype(BF16)


def layer_kernel(
    core, rows, cols, tiles_hbm, own_hbm, halo_hbm, weight, labels,
    weight_out, grads,
    tiles, columns, sums, sems,
):
    count, tile = tiles.shape[0], tiles.shape[1]
    classes, hidden = weight.shape
    padded = grads.shape[1]
    nodes = labels.shape[1]
    send = tile // 2
    partner_at = pl.multiple_of(send * (1 - core[0]), send)
    outside_at = pl.multiple_of(send * core[0], send)
    copies = [
        pltpu.make_async_copy(own_hbm, columns.at[:, 0:2], sems.at[0]),
        pltpu.make_async_copy(
            halo_hbm.at[:, :send], columns.at[:, 2, pl.ds(partner_at, send)], sems.at[1]
        ),
        pltpu.make_async_copy(
            halo_hbm.at[:, send:], columns.at[:, 2, pl.ds(outside_at, send)], sems.at[2]
        ),
    ]
    tile_copies = [
        pltpu.make_async_copy(
            tiles_hbm.at[pl.ds(start, CHUNK)],
            tiles.at[pl.ds(start, CHUNK)],
            sems.at[3 + start // CHUNK],
        )
        for start in range(0, count, CHUNK)
    ]
    for copy in copies + tile_copies:
        copy.start()

    def masked(t):
        block = tiles[t]
        none = jnp.zeros_like(block)
        first = rows[t] == 0
        return jnp.where(first, block, none), jnp.where(first, none, block)

    def column(t):
        member = cols[t] // 3
        return columns[member, cols[t] - 3 * member]

    sums[...] = jnp.zeros_like(sums)
    grads[...] = jnp.zeros_like(grads)
    for copy in copies:
        copy.wait()
    for t in range(count):
        if t % CHUNK == 0:
            tile_copies[t // CHUNK].wait()
        at = pl.ds(pl.multiple_of(rows[t] * tile, tile), tile)
        sums[at, :] += dot(tiles[t], column(t))

    total = sums[...]
    high = total.astype(BF16)
    low = (total - high.astype(F32)).astype(BF16)
    wide = jnp.concatenate(
        [weight[...].astype(F32), jnp.zeros((padded - classes, hidden), F32)], axis=0
    ).astype(BF16)
    logits = dot(wide, high, LAST) + dot(wide, low, LAST)
    kind = lax.broadcasted_iota(jnp.int32, (padded, nodes), 0)
    logits = jnp.where(kind < classes, logits, -jnp.inf)
    shifted = logits - jnp.max(logits, axis=0, keepdims=True)
    logp = shifted - jnp.log(jnp.sum(jnp.exp(shifted), axis=0, keepdims=True))
    onehot = kind == labels[...]
    losses = -jnp.sum(jnp.where(onehot, logp, 0.0), axis=0, keepdims=True)
    grad = (jnp.exp(logp) - onehot.astype(F32)).astype(BF16)

    weight_grad = dot(grad, high) + dot(grad, low)
    weight_grad = jnp.where(kind == classes, losses, weight_grad)
    weight_grad = weight_grad.astype(BF16)
    pieces = padded // PIECE
    weight_out[2 * pieces :] = jnp.zeros_like(weight_out[2 * pieces :])
    for i in range(2 * pieces):
        row, lane = i % pieces * PIECE, i // pieces * LANES
        weight_out[i] = weight_grad[row : row + PIECE, lane : lane + LANES]

    for start in range(0, count, 2):
        a, b = masked(start), masked(start + 1)
        right = jnp.concatenate([jnp.concatenate([a[i], b[i]], axis=1) for i in range(2)], axis=0)
        both = dot(grad, right)
        grads[cols[start]] += both[:, :tile]
        grads[cols[start + 1]] += both[:, tile:]


def sum_kernel(parts, out):
    summed = jnp.sum(parts[...].astype(F32), axis=0, keepdims=True)
    out[...] = jnp.broadcast_to(summed.astype(out.dtype), out.shape)


def last_kernel(
    scale, core, counts, send_lists, own, partner, outside, weight, parts,
    out, weight_grad, loss,
):
    padded = partner.shape[0]
    even = core[0] == 0
    before = jnp.where(even, outside[...], partner[...])
    after = jnp.where(even, partner[...], outside[...])
    classes = weight.shape[0]
    first, second = slots_onehot(counts, send_lists, out.shape[0])
    send = send_lists.shape[1]
    total = own[...]
    total += dot(before[:, send:], first, LAST)
    total += dot(after[:, :send], second, LAST)
    grad = total[:classes].astype(BF16)
    out[...] = dot(grad, weight[...], FIRST).astype(BF16)

    pieces = padded // PIECE
    gathered = jnp.concatenate(
        [
            jnp.concatenate([parts[pieces * h + q].astype(F32) for q in range(pieces)], axis=0)
            for h in range(2)
        ],
        axis=1,
    )
    weight_grad[...] = gathered[:classes] * scale
    loss[...] = jnp.sum(gathered[classes : classes + 1], axis=1, keepdims=True) * scale


def per_device(features, weight, tiles, tile_rows, tile_cols, send_lists, counts, labels):
    nodes, hidden = features.shape
    classes = weight.shape[1]
    send = send_lists.shape[1]
    count, tile = tiles.shape[0], tiles.shape[1]
    reps = lax.axis_size("x")
    dom = AXES[:-1]
    domains = lax.axis_size(dom)
    padded = round_up(classes + 1, PIECE)
    core = jnp.reshape(lax.axis_index("c"), (1,)).astype(jnp.int32)
    outer = [(i, i + 1) for i in range(1, domains - 1, 2)]
    outer += [(target, source) for source, target in outer]

    def exchange(to_partner, to_outside):
        return (
            lax.ppermute(to_partner, "c", [(0, 1), (1, 0)]),
            lax.ppermute(to_outside, dom, outer),
        )

    shape = jax.ShapeDtypeStruct
    weight = weight.T

    picked = pl.pallas_call(
        pick_kernel,
        out_shape=(shape((send, hidden), BF16),) * 2,
        in_specs=[smem(), smem(), vmem(), vmem()],
        out_specs=(vmem(),) * 2,
    )(core, counts, send_lists, features)
    halo = jnp.concatenate(exchange(*picked), axis=0)
    own_rows = lax.all_gather(features, "x", axis=0, tiled=True)
    halo_rows = lax.all_gather(halo, "x", axis=0)

    weight_parts, parts = pl.pallas_call(
        layer_kernel,
        out_shape=(
            shape((lax.axis_size(NEAR), PIECE, LANES), BF16),
            shape((3 * reps, padded, tile), F32),
        ),
        in_specs=[smem(), smem(), smem(), hbm(), hbm(), hbm(), vmem(), vmem()],
        out_specs=(vmem(),) * 2,
        scratch_shapes=[
            pltpu.VMEM((count, tile, tile), BF16),
            pltpu.VMEM((reps, 3, tile, hidden), BF16),
            pltpu.VMEM((nodes, hidden), F32),
            pltpu.SemaphoreType.DMA((3 + count // CHUNK,)),
        ],
        compiler_params=params(56),
    )(
        core,
        tile_rows,
        tile_cols,
        tiles,
        own_rows.reshape(reps, 2, tile, hidden),
        halo_rows,
        weight,
        labels.reshape(1, nodes),
    )

    def fold(parts, copies):
        return pl.pallas_call(
            sum_kernel,
            out_shape=shape((copies, *parts.shape[1:]), BF16),
            in_specs=[vmem()],
            out_specs=vmem(),
            compiler_params=params(4),
        )(parts)

    own = lax.psum_scatter(parts, "x", scatter_dimension=0, tiled=True)
    weight_parts = lax.all_to_all(weight_parts, NEAR, 0, 0, tiled=True)
    weight_parts = fold(weight_parts, lax.axis_size(FAR))
    weight_parts = lax.all_to_all(weight_parts, FAR, 0, 0, tiled=True)
    weight_parts = fold(weight_parts, lax.axis_size(NEAR))
    weight_parts = lax.all_to_all(weight_parts, NEAR, 0, 0, tiled=True)

    halo = own[2].astype(BF16)
    scale = 1.0 / (domains * reps * nodes)
    grad_features, weight_grad, loss = pl.pallas_call(
        lambda *refs: last_kernel(scale, *refs),
        out_shape=(
            shape((nodes, hidden), BF16),
            shape((classes, hidden), F32),
            shape((1, 1), F32),
        ),
        in_specs=[smem(), smem()] + [vmem()] * 6,
        out_specs=(vmem(),) * 3,
        compiler_params=params(4),
    )(
        core,
        counts,
        send_lists,
        jnp.concatenate([own[0], own[1]], axis=1),
        *exchange(halo, halo),
        weight,
        weight_parts,
    )
    return grad_features, weight_grad.T, loss.reshape(())


def solution(mesh):
    split = Mesh(mesh.devices.reshape(SHAPE), AXES)
    both = AXES
    placed = (
        P(both, None),
        P(),
        P(both, None, None),
        P(both),
        P(both),
        P(both, None),
        P(both),
        P(both),
    )
    return jax.shard_map(
        per_device,
        mesh=split,
        in_specs=placed,
        out_specs=(P(both, None), P(), P()),
        check_vma=False,
    )
```

```python
import jax
import jax.numpy as jnp
from jax import lax
from jax.experimental import pallas as pl
from jax.experimental.pallas import tpu as pltpu
from jax.sharding import Mesh, PartitionSpec as P

F32 = jnp.float32
BF16 = jnp.bfloat16
LANES = 128
PIECE = 16
SHAPE = (4, 2, 8, 2, 8)
AXES = ("zh", "zl", "y", "c", "x")
NEAR = ("zl", "y", "c")
FAR = ("zh", "x")
CHUNK = 32
LAST = (((1,), (1,)), ((), ()))
FIRST = (((0,), (0,)), ((), ()))
PLAIN = (((1,), (0,)), ((), ()))


def round_up(value, unit):
    return -(-value // unit) * unit


def dot(a, b, dims=PLAIN):
    return lax.dot_general(a, b, dims, preferred_element_type=F32)


def vmem():
    return pl.BlockSpec(memory_space=pltpu.VMEM)


def smem():
    return pl.BlockSpec(memory_space=pltpu.SMEM)


def hbm():
    return pl.BlockSpec(memory_space=pl.ANY)


def params(mib):
    return pltpu.CompilerParams(vmem_limit_bytes=mib * 2**20)


def slots_onehot(counts, send_lists, rows):
    send = send_lists.shape[1]
    row = lax.broadcasted_iota(jnp.int32, (rows, send), 0)
    slot = lax.broadcasted_iota(jnp.int32, (rows, send), 1)
    sides = [
        jnp.where((row == send_lists[i : i + 1, :]) & (slot < counts[i]), 1.0, 0.0)
        for i in range(2)
    ]
    return [side.astype(BF16) for side in sides]


def pick_kernel(core, counts, send_lists, features, partner, outside):
    first, second = slots_onehot(counts, send_lists, features.shape[0])
    even = core[0] == 0
    partner[...] = dot(jnp.where(even, second, first), features[...], FIRST).astype(BF16)
    outside[...] = dot(jnp.where(even, first, second), features[...], FIRST).astype(BF16)


def layer_kernel(
    core, rows_hbm, cols_hbm, tiles_hbm, own_hbm, halo_hbm, weight_hbm, labels_hbm,
    weight_out, grads,
    rows, cols, tiles, columns, weight, labels, sums, small_sems, sems,
):
    count, tile = tiles.shape[0], tiles.shape[1]
    classes, hidden = weight.shape
    padded = grads.shape[1]
    nodes = labels.shape[1]
    send = tile // 2
    partner_at = pl.multiple_of(send * (1 - core[0]), send)
    outside_at = pl.multiple_of(send * core[0], send)
    copies = [
        pltpu.make_async_copy(rows_hbm, rows, small_sems.at[0]),
        pltpu.make_async_copy(cols_hbm, cols, small_sems.at[1]),
        pltpu.make_async_copy(weight_hbm, weight, small_sems.at[2]),
        pltpu.make_async_copy(labels_hbm, labels, small_sems.at[3]),
        pltpu.make_async_copy(own_hbm, columns.at[:, 0:2], sems.at[0]),
        pltpu.make_async_copy(
            halo_hbm.at[:, :send], columns.at[:, 2, pl.ds(partner_at, send)], sems.at[1]
        ),
        pltpu.make_async_copy(
            halo_hbm.at[:, send:], columns.at[:, 2, pl.ds(outside_at, send)], sems.at[2]
        ),
    ]
    tile_copies = [
        pltpu.make_async_copy(
            tiles_hbm.at[pl.ds(start, CHUNK)],
            tiles.at[pl.ds(start, CHUNK)],
            sems.at[3 + start // CHUNK],
        )
        for start in range(0, count, CHUNK)
    ]
    for copy in copies + tile_copies:
        copy.start()

    def masked(t):
        block = tiles[t]
        none = jnp.zeros_like(block)
        first = rows[t] == 0
        return jnp.where(first, block, none), jnp.where(first, none, block)

    def column(t):
        member = cols[t] // 3
        return columns[member, cols[t] - 3 * member]

    sums[...] = jnp.zeros_like(sums)
    grads[...] = jnp.zeros_like(grads)
    for copy in copies:
        copy.wait()
    for t in range(count):
        if t % CHUNK == 0:
            tile_copies[t // CHUNK].wait()
        at = pl.ds(pl.multiple_of(rows[t] * tile, tile), tile)
        sums[at, :] += dot(tiles[t], column(t))

    total = sums[...]
    high = total.astype(BF16)
    low = (total - high.astype(F32)).astype(BF16)
    wide = jnp.concatenate(
        [weight[...].astype(F32), jnp.zeros((padded - classes, hidden), F32)], axis=0
    ).astype(BF16)
    logits = dot(wide, high, LAST) + dot(wide, low, LAST)
    kind = lax.broadcasted_iota(jnp.int32, (padded, nodes), 0)
    logits = jnp.where(kind < classes, logits, -jnp.inf)
    shifted = logits - jnp.max(logits, axis=0, keepdims=True)
    logp = shifted - jnp.log(jnp.sum(jnp.exp(shifted), axis=0, keepdims=True))
    onehot = kind == labels[...]
    losses = -jnp.sum(jnp.where(onehot, logp, 0.0), axis=0, keepdims=True)
    grad = (jnp.exp(logp) - onehot.astype(F32)).astype(BF16)

    weight_grad = dot(grad, high) + dot(grad, low)
    weight_grad = jnp.where(kind == classes, losses, weight_grad)
    weight_grad = weight_grad.astype(BF16)
    pieces = padded // PIECE
    weight_out[2 * pieces :] = jnp.zeros_like(weight_out[2 * pieces :])
    for i in range(2 * pieces):
        row, lane = i % pieces * PIECE, i // pieces * LANES
        weight_out[i] = weight_grad[row : row + PIECE, lane : lane + LANES]

    for start in range(0, count, 2):
        a, b = masked(start), masked(start + 1)
        right = jnp.concatenate([jnp.concatenate([a[i], b[i]], axis=1) for i in range(2)], axis=0)
        both = dot(grad, right)
        grads[cols[start]] += both[:, :tile]
        grads[cols[start + 1]] += both[:, tile:]


def sum_kernel(parts, out):
    summed = jnp.sum(parts[...].astype(F32), axis=0, keepdims=True)
    out[...] = jnp.broadcast_to(summed.astype(out.dtype), out.shape)


def last_kernel(
    scale, core, counts, send_lists, own, partner, outside, weight, parts,
    out, weight_grad, loss,
):
    padded = partner.shape[0]
    even = core[0] == 0
    before = jnp.where(even, outside[...], partner[...])
    after = jnp.where(even, partner[...], outside[...])
    classes = weight.shape[0]
    first, second = slots_onehot(counts, send_lists, out.shape[0])
    send = send_lists.shape[1]
    total = own[...]
    total += dot(before[:, send:], first, LAST)
    total += dot(after[:, :send], second, LAST)
    grad = total[:classes].astype(BF16)
    out[...] = dot(grad, weight[...], FIRST).astype(BF16)

    pieces = padded // PIECE
    gathered = jnp.concatenate(
        [
            jnp.concatenate([parts[pieces * h + q].astype(F32) for q in range(pieces)], axis=0)
            for h in range(2)
        ],
        axis=1,
    )
    weight_grad[...] = gathered[:classes] * scale
    loss[...] = jnp.sum(gathered[classes : classes + 1], axis=1, keepdims=True) * scale


def per_device(features, weight, tiles, tile_rows, tile_cols, send_lists, counts, labels):
    nodes, hidden = features.shape
    classes = weight.shape[1]
    send = send_lists.shape[1]
    count, tile = tiles.shape[0], tiles.shape[1]
    reps = lax.axis_size("x")
    dom = AXES[:-1]
    domains = lax.axis_size(dom)
    padded = round_up(classes + 1, PIECE)
    core = jnp.reshape(lax.axis_index("c"), (1,)).astype(jnp.int32)
    outer = [(i, i + 1) for i in range(1, domains - 1, 2)]
    outer += [(target, source) for source, target in outer]

    def exchange(to_partner, to_outside):
        return (
            lax.ppermute(to_partner, "c", [(0, 1), (1, 0)]),
            lax.ppermute(to_outside, dom, outer),
        )

    shape = jax.ShapeDtypeStruct
    weight = weight.T

    picked = pl.pallas_call(
        pick_kernel,
        out_shape=(shape((send, hidden), BF16),) * 2,
        in_specs=[smem(), smem(), vmem(), vmem()],
        out_specs=(vmem(),) * 2,
    )(core, counts, send_lists, features)
    halo = jnp.concatenate(exchange(*picked), axis=0)
    own_rows = lax.all_gather(features, "x", axis=0, tiled=True)
    halo_rows = lax.all_gather(halo, "x", axis=0)

    weight_parts, parts = pl.pallas_call(
        layer_kernel,
        out_shape=(
            shape((lax.axis_size(NEAR), PIECE, LANES), BF16),
            shape((3 * reps, padded, tile), F32),
        ),
        in_specs=[smem()] + [hbm()] * 7,
        out_specs=(vmem(),) * 2,
        scratch_shapes=[
            pltpu.SMEM((count,), jnp.int32),
            pltpu.SMEM((count,), jnp.int32),
            pltpu.VMEM((count, tile, tile), BF16),
            pltpu.VMEM((reps, 3, tile, hidden), BF16),
            pltpu.VMEM((classes, hidden), BF16),
            pltpu.VMEM((1, nodes), jnp.int32),
            pltpu.VMEM((nodes, hidden), F32),
            pltpu.SemaphoreType.DMA((4,)),
            pltpu.SemaphoreType.DMA((3 + count // CHUNK,)),
        ],
        compiler_params=params(56),
    )(
        core,
        tile_rows,
        tile_cols,
        tiles,
        own_rows.reshape(reps, 2, tile, hidden),
        halo_rows,
        weight,
        labels.reshape(1, nodes),
    )

    def fold(parts, copies):
        return pl.pallas_call(
            sum_kernel,
            out_shape=shape((copies, *parts.shape[1:]), BF16),
            in_specs=[vmem()],
            out_specs=vmem(),
            compiler_params=params(4),
        )(parts)

    own = lax.psum_scatter(parts, "x", scatter_dimension=0, tiled=True)
    weight_parts = lax.all_to_all(weight_parts, NEAR, 0, 0, tiled=True)
    weight_parts = fold(weight_parts, lax.axis_size(FAR))
    weight_parts = lax.all_to_all(weight_parts, FAR, 0, 0, tiled=True)
    weight_parts = fold(weight_parts, lax.axis_size(NEAR))
    weight_parts = lax.all_to_all(weight_parts, NEAR, 0, 0, tiled=True)

    halo = own[2].astype(BF16)
    scale = 1.0 / (domains * reps * nodes)
    grad_features, weight_grad, loss = pl.pallas_call(
        lambda *refs: last_kernel(scale, *refs),
        out_shape=(
            shape((nodes, hidden), BF16),
            shape((classes, hidden), F32),
            shape((1, 1), F32),
        ),
        in_specs=[smem(), smem()] + [vmem()] * 6,
        out_specs=(vmem(),) * 3,
        compiler_params=params(4),
    )(
        core,
        counts,
        send_lists,
        jnp.concatenate([own[0], own[1]], axis=1),
        *exchange(halo, halo),
        weight,
        weight_parts,
    )
    return grad_features, weight_grad.T, loss.reshape(())


def solution(mesh):
    split = Mesh(mesh.devices.reshape(SHAPE), AXES)
    both = AXES
    placed = (
        P(both, None),
        P(),
        P(both, None, None),
        P(both),
        P(both),
        P(both, None),
        P(both),
        P(both),
    )
    return jax.shard_map(
        per_device,
        mesh=split,
        in_specs=placed,
        out_specs=(P(both, None), P(), P()),
        check_vma=False,
    )
```

```python
import jax
import jax.numpy as jnp
from jax import lax
from jax.experimental import pallas as pl
from jax.experimental.pallas import tpu as pltpu
from jax.sharding import Mesh, PartitionSpec as P

F32 = jnp.float32
BF16 = jnp.bfloat16
LANES = 128
PIECE = 16
SHAPE = (4, 2, 8, 2, 8)
AXES = ("zh", "zl", "y", "c", "x")
NEAR = ("zl", "c", "x")
FAR = ("zh", "y")
CHUNK = 32
LAST = (((1,), (1,)), ((), ()))
FIRST = (((0,), (0,)), ((), ()))
PLAIN = (((1,), (0,)), ((), ()))


def round_up(value, unit):
    return -(-value // unit) * unit


def dot(a, b, dims=PLAIN):
    return lax.dot_general(a, b, dims, preferred_element_type=F32)


def vmem():
    return pl.BlockSpec(memory_space=pltpu.VMEM)


def smem():
    return pl.BlockSpec(memory_space=pltpu.SMEM)


def hbm():
    return pl.BlockSpec(memory_space=pl.ANY)


def params(mib):
    return pltpu.CompilerParams(vmem_limit_bytes=mib * 2**20)


def slots_onehot(counts, send_lists, rows):
    send = send_lists.shape[1]
    row = lax.broadcasted_iota(jnp.int32, (rows, send), 0)
    slot = lax.broadcasted_iota(jnp.int32, (rows, send), 1)
    sides = [
        jnp.where((row == send_lists[i : i + 1, :]) & (slot < counts[i]), 1.0, 0.0)
        for i in range(2)
    ]
    return [side.astype(BF16) for side in sides]


def pick_kernel(core, counts, send_lists, features, partner, outside):
    first, second = slots_onehot(counts, send_lists, features.shape[0])
    even = core[0] == 0
    partner[...] = dot(jnp.where(even, second, first), features[...], FIRST).astype(BF16)
    outside[...] = dot(jnp.where(even, first, second), features[...], FIRST).astype(BF16)


def layer_kernel(
    core, rows_hbm, cols_hbm, tiles_hbm, own_hbm, halo_hbm, weight_hbm, labels_hbm,
    weight_out, grads,
    rows, cols, tiles, columns, weight, labels, sums, small_sems, sems,
):
    count, tile = tiles.shape[0], tiles.shape[1]
    classes, hidden = weight.shape
    padded = grads.shape[1]
    nodes = labels.shape[1]
    send = tile // 2
    partner_at = pl.multiple_of(send * (1 - core[0]), send)
    outside_at = pl.multiple_of(send * core[0], send)
    copies = [
        pltpu.make_async_copy(rows_hbm, rows, small_sems.at[0]),
        pltpu.make_async_copy(cols_hbm, cols, small_sems.at[1]),
        pltpu.make_async_copy(weight_hbm, weight, small_sems.at[2]),
        pltpu.make_async_copy(labels_hbm, labels, small_sems.at[3]),
        pltpu.make_async_copy(own_hbm, columns.at[:, 0:2], sems.at[0]),
        pltpu.make_async_copy(
            halo_hbm.at[:, :send], columns.at[:, 2, pl.ds(partner_at, send)], sems.at[1]
        ),
        pltpu.make_async_copy(
            halo_hbm.at[:, send:], columns.at[:, 2, pl.ds(outside_at, send)], sems.at[2]
        ),
    ]
    tile_copies = [
        pltpu.make_async_copy(
            tiles_hbm.at[pl.ds(start, CHUNK)],
            tiles.at[pl.ds(start, CHUNK)],
            sems.at[3 + start // CHUNK],
        )
        for start in range(0, count, CHUNK)
    ]
    for copy in copies + tile_copies:
        copy.start()

    def masked(t):
        block = tiles[t]
        none = jnp.zeros_like(block)
        first = rows[t] == 0
        return jnp.where(first, block, none), jnp.where(first, none, block)

    def column(t):
        member = cols[t] // 3
        return columns[member, cols[t] - 3 * member]

    sums[...] = jnp.zeros_like(sums)
    grads[...] = jnp.zeros_like(grads)
    for copy in copies:
        copy.wait()
    for t in range(count):
        if t % CHUNK == 0:
            tile_copies[t // CHUNK].wait()
        at = pl.ds(pl.multiple_of(rows[t] * tile, tile), tile)
        sums[at, :] += dot(tiles[t], column(t))

    total = sums[...]
    high = total.astype(BF16)
    low = (total - high.astype(F32)).astype(BF16)
    wide = jnp.concatenate(
        [weight[...].astype(F32), jnp.zeros((padded - classes, hidden), F32)], axis=0
    ).astype(BF16)
    logits = dot(wide, high, LAST) + dot(wide, low, LAST)
    kind = lax.broadcasted_iota(jnp.int32, (padded, nodes), 0)
    logits = jnp.where(kind < classes, logits, -jnp.inf)
    shifted = logits - jnp.max(logits, axis=0, keepdims=True)
    logp = shifted - jnp.log(jnp.sum(jnp.exp(shifted), axis=0, keepdims=True))
    onehot = kind == labels[...]
    losses = -jnp.sum(jnp.where(onehot, logp, 0.0), axis=0, keepdims=True)
    grad = (jnp.exp(logp) - onehot.astype(F32)).astype(BF16)

    weight_grad = dot(grad, high) + dot(grad, low)
    weight_grad = jnp.where(kind == classes, losses, weight_grad)
    weight_grad = weight_grad.astype(BF16)
    pieces = padded // PIECE
    weight_out[2 * pieces :] = jnp.zeros_like(weight_out[2 * pieces :])
    for i in range(2 * pieces):
        row, lane = i % pieces * PIECE, i // pieces * LANES
        weight_out[i] = weight_grad[row : row + PIECE, lane : lane + LANES]

    for start in range(0, count, 2):
        a, b = masked(start), masked(start + 1)
        right = jnp.concatenate([jnp.concatenate([a[i], b[i]], axis=1) for i in range(2)], axis=0)
        both = dot(grad, right)
        grads[cols[start]] += both[:, :tile]
        grads[cols[start + 1]] += both[:, tile:]


def sum_kernel(parts, out):
    summed = jnp.sum(parts[...].astype(F32), axis=0, keepdims=True)
    out[...] = jnp.broadcast_to(summed.astype(out.dtype), out.shape)


def last_kernel(
    scale, core, counts, send_lists, own, partner, outside, weight, parts,
    out, weight_grad, loss,
):
    padded = partner.shape[0]
    even = core[0] == 0
    before = jnp.where(even, outside[...], partner[...])
    after = jnp.where(even, partner[...], outside[...])
    classes = weight.shape[0]
    first, second = slots_onehot(counts, send_lists, out.shape[0])
    send = send_lists.shape[1]
    total = own[...]
    total += dot(before[:, send:], first, LAST)
    total += dot(after[:, :send], second, LAST)
    grad = total[:classes].astype(BF16)
    out[...] = dot(grad, weight[...], FIRST).astype(BF16)

    pieces = padded // PIECE
    gathered = jnp.concatenate(
        [
            jnp.concatenate([parts[pieces * h + q].astype(F32) for q in range(pieces)], axis=0)
            for h in range(2)
        ],
        axis=1,
    )
    weight_grad[...] = gathered[:classes] * scale
    loss[...] = jnp.sum(gathered[classes : classes + 1], axis=1, keepdims=True) * scale


def per_device(features, weight, tiles, tile_rows, tile_cols, send_lists, counts, labels):
    nodes, hidden = features.shape
    classes = weight.shape[1]
    send = send_lists.shape[1]
    count, tile = tiles.shape[0], tiles.shape[1]
    reps = lax.axis_size("x")
    dom = AXES[:-1]
    domains = lax.axis_size(dom)
    padded = round_up(classes + 1, PIECE)
    core = jnp.reshape(lax.axis_index("c"), (1,)).astype(jnp.int32)
    outer = [(i, i + 1) for i in range(1, domains - 1, 2)]
    outer += [(target, source) for source, target in outer]

    def exchange(to_partner, to_outside):
        return (
            lax.ppermute(to_partner, "c", [(0, 1), (1, 0)]),
            lax.ppermute(to_outside, dom, outer),
        )

    shape = jax.ShapeDtypeStruct
    weight = weight.T

    picked = pl.pallas_call(
        pick_kernel,
        out_shape=(shape((send, hidden), BF16),) * 2,
        in_specs=[smem(), smem(), vmem(), vmem()],
        out_specs=(vmem(),) * 2,
    )(core, counts, send_lists, features)
    halo = jnp.concatenate(exchange(*picked), axis=0)
    own_rows = lax.all_gather(features, "x", axis=0, tiled=True)
    halo_rows = lax.all_gather(halo, "x", axis=0)

    weight_parts, parts = pl.pallas_call(
        layer_kernel,
        out_shape=(
            shape((lax.axis_size(NEAR), PIECE, LANES), BF16),
            shape((3 * reps, padded, tile), F32),
        ),
        in_specs=[smem()] + [hbm()] * 7,
        out_specs=(vmem(),) * 2,
        scratch_shapes=[
            pltpu.SMEM((count,), jnp.int32),
            pltpu.SMEM((count,), jnp.int32),
            pltpu.VMEM((count, tile, tile), BF16),
            pltpu.VMEM((reps, 3, tile, hidden), BF16),
            pltpu.VMEM((classes, hidden), BF16),
            pltpu.VMEM((1, nodes), jnp.int32),
            pltpu.VMEM((nodes, hidden), F32),
            pltpu.SemaphoreType.DMA((4,)),
            pltpu.SemaphoreType.DMA((3 + count // CHUNK,)),
        ],
        compiler_params=params(56),
    )(
        core,
        tile_rows,
        tile_cols,
        tiles,
        own_rows.reshape(reps, 2, tile, hidden),
        halo_rows,
        weight,
        labels.reshape(1, nodes),
    )

    def fold(parts, copies):
        return pl.pallas_call(
            sum_kernel,
            out_shape=shape((copies, *parts.shape[1:]), BF16),
            in_specs=[vmem()],
            out_specs=vmem(),
            compiler_params=params(4),
        )(parts)

    own = lax.psum_scatter(parts, "x", scatter_dimension=0, tiled=True)
    weight_parts = lax.all_to_all(weight_parts, NEAR, 0, 0, tiled=True)
    weight_parts = fold(weight_parts, lax.axis_size(FAR))
    weight_parts = lax.all_to_all(weight_parts, FAR, 0, 0, tiled=True)
    weight_parts = fold(weight_parts, lax.axis_size(NEAR))
    weight_parts = lax.all_to_all(weight_parts, NEAR, 0, 0, tiled=True)

    halo = own[2].astype(BF16)
    scale = 1.0 / (domains * reps * nodes)
    grad_features, weight_grad, loss = pl.pallas_call(
        lambda *refs: last_kernel(scale, *refs),
        out_shape=(
            shape((nodes, hidden), BF16),
            shape((classes, hidden), F32),
            shape((1, 1), F32),
        ),
        in_specs=[smem(), smem()] + [vmem()] * 6,
        out_specs=(vmem(),) * 3,
        compiler_params=params(4),
    )(
        core,
        counts,
        send_lists,
        jnp.concatenate([own[0], own[1]], axis=1),
        *exchange(halo, halo),
        weight,
        weight_parts,
    )
    return grad_features, weight_grad.T, loss.reshape(())


def solution(mesh):
    split = Mesh(mesh.devices.reshape(SHAPE), AXES)
    both = AXES
    placed = (
        P(both, None),
        P(),
        P(both, None, None),
        P(both),
        P(both),
        P(both, None),
        P(both),
        P(both),
    )
    return jax.shard_map(
        per_device,
        mesh=split,
        in_specs=placed,
        out_specs=(P(both, None), P(), P()),
        check_vma=False,
    )
```

```python
import jax
import jax.numpy as jnp
from jax import lax
from jax.experimental import pallas as pl
from jax.experimental.pallas import tpu as pltpu
from jax.sharding import Mesh, PartitionSpec as P

F32 = jnp.float32
BF16 = jnp.bfloat16
LANES = 128
PIECE = 16
SHAPE = (4, 2, 8, 2, 8)
AXES = ("zh", "zl", "y", "c", "x")
NEAR = ("zl", "c", "x")
FAR = ("zh", "y")
CHUNK = 64
LAST = (((1,), (1,)), ((), ()))
FIRST = (((0,), (0,)), ((), ()))
PLAIN = (((1,), (0,)), ((), ()))


def round_up(value, unit):
    return -(-value // unit) * unit


def dot(a, b, dims=PLAIN):
    return lax.dot_general(a, b, dims, preferred_element_type=F32)


def vmem():
    return pl.BlockSpec(memory_space=pltpu.VMEM)


def smem():
    return pl.BlockSpec(memory_space=pltpu.SMEM)


def hbm():
    return pl.BlockSpec(memory_space=pl.ANY)


def params(mib):
    return pltpu.CompilerParams(vmem_limit_bytes=mib * 2**20)


def slots_onehot(counts, send_lists, rows):
    send = send_lists.shape[1]
    row = lax.broadcasted_iota(jnp.int32, (rows, send), 0)
    slot = lax.broadcasted_iota(jnp.int32, (rows, send), 1)
    sides = [
        jnp.where((row == send_lists[i : i + 1, :]) & (slot < counts[i]), 1.0, 0.0)
        for i in range(2)
    ]
    return [side.astype(BF16) for side in sides]


def pick_kernel(core, counts, send_lists, features, partner, outside):
    first, second = slots_onehot(counts, send_lists, features.shape[0])
    even = core[0] == 0
    partner[...] = dot(jnp.where(even, second, first), features[...], FIRST).astype(BF16)
    outside[...] = dot(jnp.where(even, first, second), features[...], FIRST).astype(BF16)


def layer_kernel(
    core, rows_hbm, cols_hbm, tiles_hbm, own_hbm, halo_hbm, weight_hbm, labels_hbm,
    weight_out, grads,
    rows, cols, tiles, columns, weight, labels, sums, small_sems, sems,
):
    count, tile = tiles.shape[0], tiles.shape[1]
    classes, hidden = weight.shape
    padded = grads.shape[1]
    nodes = labels.shape[1]
    send = tile // 2
    partner_at = pl.multiple_of(send * (1 - core[0]), send)
    outside_at = pl.multiple_of(send * core[0], send)
    copies = [
        pltpu.make_async_copy(rows_hbm, rows, small_sems.at[0]),
        pltpu.make_async_copy(cols_hbm, cols, small_sems.at[1]),
        pltpu.make_async_copy(weight_hbm, weight, small_sems.at[2]),
        pltpu.make_async_copy(labels_hbm, labels, small_sems.at[3]),
        pltpu.make_async_copy(own_hbm, columns.at[:, 0:2], sems.at[0]),
        pltpu.make_async_copy(
            halo_hbm.at[:, :send], columns.at[:, 2, pl.ds(partner_at, send)], sems.at[1]
        ),
        pltpu.make_async_copy(
            halo_hbm.at[:, send:], columns.at[:, 2, pl.ds(outside_at, send)], sems.at[2]
        ),
    ]
    tile_copies = [
        pltpu.make_async_copy(
            tiles_hbm.at[pl.ds(start, CHUNK)],
            tiles.at[pl.ds(start, CHUNK)],
            sems.at[3 + start // CHUNK],
        )
        for start in range(0, count, CHUNK)
    ]
    for copy in copies + tile_copies:
        copy.start()

    def masked(t):
        block = tiles[t]
        none = jnp.zeros_like(block)
        first = rows[t] == 0
        return jnp.where(first, block, none), jnp.where(first, none, block)

    def column(t):
        member = cols[t] // 3
        return columns[member, cols[t] - 3 * member]

    sums[...] = jnp.zeros_like(sums)
    grads[...] = jnp.zeros_like(grads)
    for copy in copies:
        copy.wait()
    for t in range(count):
        if t % CHUNK == 0:
            tile_copies[t // CHUNK].wait()
        at = pl.ds(pl.multiple_of(rows[t] * tile, tile), tile)
        sums[at, :] += dot(tiles[t], column(t))

    total = sums[...]
    high = total.astype(BF16)
    low = (total - high.astype(F32)).astype(BF16)
    wide = jnp.concatenate(
        [weight[...].astype(F32), jnp.zeros((padded - classes, hidden), F32)], axis=0
    ).astype(BF16)
    logits = dot(wide, high, LAST) + dot(wide, low, LAST)
    kind = lax.broadcasted_iota(jnp.int32, (padded, nodes), 0)
    logits = jnp.where(kind < classes, logits, -jnp.inf)
    shifted = logits - jnp.max(logits, axis=0, keepdims=True)
    logp = shifted - jnp.log(jnp.sum(jnp.exp(shifted), axis=0, keepdims=True))
    onehot = kind == labels[...]
    losses = -jnp.sum(jnp.where(onehot, logp, 0.0), axis=0, keepdims=True)
    grad = (jnp.exp(logp) - onehot.astype(F32)).astype(BF16)

    weight_grad = dot(grad, high) + dot(grad, low)
    weight_grad = jnp.where(kind == classes, losses, weight_grad)
    weight_grad = weight_grad.astype(BF16)
    pieces = padded // PIECE
    weight_out[2 * pieces :] = jnp.zeros_like(weight_out[2 * pieces :])
    for i in range(2 * pieces):
        row, lane = i % pieces * PIECE, i // pieces * LANES
        weight_out[i] = weight_grad[row : row + PIECE, lane : lane + LANES]

    for start in range(0, count, 2):
        a, b = masked(start), masked(start + 1)
        right = jnp.concatenate([jnp.concatenate([a[i], b[i]], axis=1) for i in range(2)], axis=0)
        both = dot(grad, right)
        grads[cols[start]] += both[:, :tile]
        grads[cols[start + 1]] += both[:, tile:]


def sum_kernel(parts, out):
    summed = jnp.sum(parts[...].astype(F32), axis=0, keepdims=True)
    out[...] = jnp.broadcast_to(summed.astype(out.dtype), out.shape)


def last_kernel(
    scale, core, counts, send_lists, own, partner, outside, weight, parts,
    out, weight_grad, loss,
):
    padded = partner.shape[0]
    even = core[0] == 0
    before = jnp.where(even, outside[...], partner[...])
    after = jnp.where(even, partner[...], outside[...])
    classes = weight.shape[0]
    first, second = slots_onehot(counts, send_lists, out.shape[0])
    send = send_lists.shape[1]
    total = own[...]
    total += dot(before[:, send:], first, LAST)
    total += dot(after[:, :send], second, LAST)
    grad = total[:classes].astype(BF16)
    out[...] = dot(grad, weight[...], FIRST).astype(BF16)

    pieces = padded // PIECE
    gathered = jnp.concatenate(
        [
            jnp.concatenate([parts[pieces * h + q].astype(F32) for q in range(pieces)], axis=0)
            for h in range(2)
        ],
        axis=1,
    )
    weight_grad[...] = gathered[:classes] * scale
    loss[...] = jnp.sum(gathered[classes : classes + 1], axis=1, keepdims=True) * scale


def per_device(features, weight, tiles, tile_rows, tile_cols, send_lists, counts, labels):
    nodes, hidden = features.shape
    classes = weight.shape[1]
    send = send_lists.shape[1]
    count, tile = tiles.shape[0], tiles.shape[1]
    reps = lax.axis_size("x")
    dom = AXES[:-1]
    domains = lax.axis_size(dom)
    padded = round_up(classes + 1, PIECE)
    core = jnp.reshape(lax.axis_index("c"), (1,)).astype(jnp.int32)
    outer = [(i, i + 1) for i in range(1, domains - 1, 2)]
    outer += [(target, source) for source, target in outer]

    def exchange(to_partner, to_outside):
        return (
            lax.ppermute(to_partner, "c", [(0, 1), (1, 0)]),
            lax.ppermute(to_outside, dom, outer),
        )

    shape = jax.ShapeDtypeStruct
    weight = weight.T

    picked = pl.pallas_call(
        pick_kernel,
        out_shape=(shape((send, hidden), BF16),) * 2,
        in_specs=[smem(), smem(), vmem(), vmem()],
        out_specs=(vmem(),) * 2,
    )(core, counts, send_lists, features)
    halo = jnp.concatenate(exchange(*picked), axis=0)
    own_rows = lax.all_gather(features, "x", axis=0, tiled=True)
    halo_rows = lax.all_gather(halo, "x", axis=0)

    weight_parts, parts = pl.pallas_call(
        layer_kernel,
        out_shape=(
            shape((lax.axis_size(NEAR), PIECE, LANES), BF16),
            shape((3 * reps, padded, tile), F32),
        ),
        in_specs=[smem()] + [hbm()] * 7,
        out_specs=(vmem(),) * 2,
        scratch_shapes=[
            pltpu.SMEM((count,), jnp.int32),
            pltpu.SMEM((count,), jnp.int32),
            pltpu.VMEM((count, tile, tile), BF16),
            pltpu.VMEM((reps, 3, tile, hidden), BF16),
            pltpu.VMEM((classes, hidden), BF16),
            pltpu.VMEM((1, nodes), jnp.int32),
            pltpu.VMEM((nodes, hidden), F32),
            pltpu.SemaphoreType.DMA((4,)),
            pltpu.SemaphoreType.DMA((3 + count // CHUNK,)),
        ],
        compiler_params=params(56),
    )(
        core,
        tile_rows,
        tile_cols,
        tiles,
        own_rows.reshape(reps, 2, tile, hidden),
        halo_rows,
        weight,
        labels.reshape(1, nodes),
    )

    def fold(parts, copies):
        return pl.pallas_call(
            sum_kernel,
            out_shape=shape((copies, *parts.shape[1:]), BF16),
            in_specs=[vmem()],
            out_specs=vmem(),
            compiler_params=params(4),
        )(parts)

    own = lax.psum_scatter(parts, "x", scatter_dimension=0, tiled=True)
    weight_parts = lax.all_to_all(weight_parts, NEAR, 0, 0, tiled=True)
    weight_parts = fold(weight_parts, lax.axis_size(FAR))
    weight_parts = lax.all_to_all(weight_parts, FAR, 0, 0, tiled=True)
    weight_parts = fold(weight_parts, lax.axis_size(NEAR))
    weight_parts = lax.all_to_all(weight_parts, NEAR, 0, 0, tiled=True)

    halo = own[2].astype(BF16)
    scale = 1.0 / (domains * reps * nodes)
    grad_features, weight_grad, loss = pl.pallas_call(
        lambda *refs: last_kernel(scale, *refs),
        out_shape=(
            shape((nodes, hidden), BF16),
            shape((classes, hidden), F32),
            shape((1, 1), F32),
        ),
        in_specs=[smem(), smem()] + [vmem()] * 6,
        out_specs=(vmem(),) * 3,
        compiler_params=params(4),
    )(
        core,
        counts,
        send_lists,
        jnp.concatenate([own[0], own[1]], axis=1),
        *exchange(halo, halo),
        weight,
        weight_parts,
    )
    return grad_features, weight_grad.T, loss.reshape(())


def solution(mesh):
    split = Mesh(mesh.devices.reshape(SHAPE), AXES)
    both = AXES
    placed = (
        P(both, None),
        P(),
        P(both, None, None),
        P(both),
        P(both),
        P(both, None),
        P(both),
        P(both),
    )
    return jax.shard_map(
        per_device,
        mesh=split,
        in_specs=placed,
        out_specs=(P(both, None), P(), P()),
        check_vma=False,
    )
```
